32 devices in a mesh: grp: 2 (over x), tile: 16 (over z, y, core).
Axes of the slice: x: 2, y: 2, z: 4, core: 2. Of those that a mesh axis runs over, the one named last changes fastest.
Arguments:
- object_field: float32 [2, 1280, 2048], P(None, ('grp', 'tile')), parts along dimension 1, may hold values from -6 to 6
- probe_modes: float32 [2, 8, 256, 256], P(None, 'grp'), parts along dimension 1, may hold values from -3 to 3
- positions: int32 [128, 2], P(('grp', 'tile')), parts along dimension 0, may hold values from 0 to 1792, as said below
- intensity: float32 [128, 256, 256], P(('grp', 'tile')), parts along dimension 0, may hold values from 0.5 to 20
Outputs:
- object_step: float32 [2, 1280, 2048], P(None, ('grp', 'tile')), parts along dimension 1
- probe_step: float32 [2, 8, 256, 256], P(None, 'grp'), parts along dimension 1
The draws below stay inside these ranges and needn't reach their ends.
There are 2 independent parts, one for each index of `grp`. The reference program is written for one: setup_inputs(seed, part) draws one part's arguments, and reference() takes and returns one part's arrays. A program takes and returns all parts, laid end to end along the dimension named above; each array names one. Nothing has to cross between parts.
Inputs may be any that keep to these rules, and one draw needn't show every extreme that they name: positions[:, 0] is a patch's corner row y and positions[:, 1] its corner column x. Position rows d * 4 to (d + 1) * 4 - 1 are held by index d of tile, and such a patch lies within object rows (d - 6) * 40 to (d + 7) * 40 - 1; y + 256 <= 640 and x + 256 <= 2048.
All inputs are finite; a program needn't handle non-finite values.
Results may differ from the reference program's by a relative error of at most 0.0077.
Values may be sent and summed in bfloat16 or wider, within the bound.
No kernel may reach another device: no remote copies, remote signals or barrier semaphores. Data moves between devices by JAX's collectives and lax.ppermute only.
A program may use at most 128 MiB of HBM per device.

```python
import math
import jax
import jax.numpy as jnp
from jax import lax

PATCH = 256
MODES = 4
TILE_ROWS = 40
W = 2048
POS_DEV = 4
REACH = 6
NY = 640
POSITIONS = 64


def draw_positions(key, part):
    key = jax.random.fold_in(key, 7)
    row_key, col_key = jax.random.split(key)
    number = jnp.arange(POSITIONS, dtype=jnp.int32)
    holder = number // POS_DEV
    slot_index = number % POS_DEV
    low_start = (holder - REACH) * TILE_ROWS
    high_start = (holder + REACH + 1) * TILE_ROWS - PATCH
    span_count = (2 * REACH + 1) * TILE_ROWS - PATCH + 1
    jitter = jax.random.randint(row_key, (POSITIONS,), 0, span_count, dtype=jnp.int32)
    row_start = low_start + jitter
    even_holder = holder % 2 == 0
    first_start = jnp.where(even_holder, low_start, high_start)
    last_start = jnp.where(even_holder, high_start, low_start)
    row_start = jnp.where(slot_index == POS_DEV - 1, last_start, row_start)
    row_start = jnp.where(slot_index == 0, first_start, row_start)
    row_start = jnp.clip(row_start, 0, NY - PATCH)
    col_start = jax.random.randint(col_key, (POSITIONS,), 0, W - PATCH + 1, dtype=jnp.int32)
    col_start = jnp.where(number == 0, W - PATCH, col_start)
    return jnp.stack([row_start, col_start], axis=1).astype(jnp.int32)


def steps_of(own_key, dims, cuts, smallest, high):
    loudness, own = 1.0, jax.random.fold_in(own_key, 6)
    for axis_at, blocks in cuts:
        heights = jnp.exp(jax.random.uniform(jax.random.fold_in(own, axis_at), (blocks,), jnp.float32, smallest / len(cuts), high / len(cuts)))
        loudness = loudness * jnp.repeat(heights, dims[axis_at] // blocks).reshape([-1 if axis == axis_at else 1 for axis in range(len(dims))])
    return loudness


def gaussian(rng, extent, spread, bound, pieces=(), kind=jnp.bfloat16):
    values = spread * jax.random.normal(rng, extent, jnp.float32)
    if pieces:
        values = values * steps_of(rng, extent, pieces, -0.22, 0.18)
    return jnp.clip(values, -bound, bound).astype(kind)


def setup_inputs(seed: int = 0, part: int = 0) -> dict:
    arg_keys = jax.random.split(jax.random.key(seed), 5)
    part_splits = jax.random.split(jax.random.fold_in(arg_keys[4], part), 5)
    object_field = gaussian(part_splits[0], (2, NY, W), 1.0, 6.0, ((1, 16),), jnp.float32)
    probe_modes = gaussian(part_splits[1], (2, MODES, PATCH, PATCH), 0.5, 3.0, (), jnp.float32)
    positions = draw_positions(jax.random.fold_in(jax.random.fold_in(arg_keys[4], part), 71), part)
    intensity = jnp.clip(jnp.exp(math.log(20.0) - 3.6888795 * jax.random.uniform(part_splits[3], (POSITIONS, PATCH, PATCH), jnp.float32) ** steps_of(part_splits[3], (POSITIONS, PATCH, PATCH), ((0, 16),), -0.2, 0.2)), 0.5, 20.0)
    return {"object_field": object_field, "probe_modes": probe_modes, "positions": positions, "intensity": intensity}


def tables(size):
    steps = jnp.arange(size, dtype=jnp.int32)
    product = steps[:, None] * steps[None, :] % size
    phase = product.astype(jnp.float32) * (2.0 * math.pi / size)
    factor = 1.0 / math.sqrt(size)
    return ((jnp.cos(phase) * factor).astype(jnp.bfloat16), (jnp.sin(phase) * factor).astype(jnp.bfloat16))

def matmul_right(left_part, table):
    return jnp.einsum('...ij,jk->...ik', left_part.astype(jnp.float32), table.astype(jnp.float32))

def matmul_left(table, right_part):
    return jnp.einsum('ij,...jk->...ik', table.astype(jnp.float32), right_part.astype(jnp.float32))

def apply_right(real_part, imag_part, cos_table, sine_table, sign):
    real_out = matmul_right(real_part, cos_table) - sign * matmul_right(imag_part, sine_table)
    imag_out = matmul_right(imag_part, cos_table) + sign * matmul_right(real_part, sine_table)
    return (real_out, imag_out)

def apply_left(real_part, imag_part, cos_table, sine_table, sign):
    real_out = matmul_left(cos_table, real_part) - sign * matmul_left(sine_table, imag_part)
    imag_out = matmul_left(cos_table, imag_part) + sign * matmul_left(sine_table, real_part)
    return (real_out, imag_out)

def one_position(patch_low, measured, probe_modes, cos_table, sine_table):
    obj_real = patch_low[0].astype(jnp.float32)
    obj_imag = patch_low[1].astype(jnp.float32)
    probe_real = probe_modes[0]
    probe_imag = probe_modes[1]
    exit_real = (probe_real * obj_real - probe_imag * obj_imag).astype(jnp.bfloat16)
    exit_imag = (probe_real * obj_imag + probe_imag * obj_real).astype(jnp.bfloat16)
    half_real, half_imag = apply_right(exit_real, exit_imag, cos_table, sine_table, -1.0)
    half_real = half_real.astype(jnp.bfloat16)
    half_imag = half_imag.astype(jnp.bfloat16)
    far_real, far_imag = apply_left(half_real, half_imag, cos_table, sine_table, -1.0)
    model = 1.0 + lax.optimization_barrier(jnp.sum(far_real * far_real + far_imag * far_imag, axis=0))
    factor = jnp.sqrt(measured / model) - 1.0
    upd_real = (far_real * factor).astype(jnp.bfloat16)
    upd_imag = (far_imag * factor).astype(jnp.bfloat16)
    back_real, back_imag = apply_right(upd_real, upd_imag, cos_table, sine_table, 1.0)
    back_real = back_real.astype(jnp.bfloat16)
    back_imag = back_imag.astype(jnp.bfloat16)
    change_real, change_imag = apply_left(back_real, back_imag, cos_table, sine_table, 1.0)
    grad_real = lax.optimization_barrier(jnp.sum(probe_real * change_real + probe_imag * change_imag, axis=0))
    grad_imag = lax.optimization_barrier(jnp.sum(probe_real * change_imag - probe_imag * change_real, axis=0))
    pgrad_real = obj_real * change_real + obj_imag * change_imag
    pgrad_imag = obj_real * change_imag - obj_imag * change_real
    power = obj_real * obj_real + obj_imag * obj_imag
    return (grad_real, grad_imag, pgrad_real, pgrad_imag, power)

def reference(object_field, probe_modes, positions, intensity):
    cos_table, sine_table = tables(PATCH)
    object_low = object_field.astype(jnp.bfloat16)
    coverage_patch = lax.optimization_barrier(jnp.sum(probe_modes[0] * probe_modes[0] + probe_modes[1] * probe_modes[1], axis=0))
    anchor = jnp.zeros((), jnp.int32)

    def visit(position, carry):
        object_sum, probe_sum, patch_power = carry
        row_start = positions[position, 0].astype(jnp.int32)
        col_start = positions[position, 1].astype(jnp.int32)
        patch_low = lax.dynamic_slice(object_low, (anchor, row_start, col_start), (2, PATCH, PATCH))
        grad_real, grad_imag, pgrad_real, pgrad_imag, power = one_position(patch_low, intensity[position], probe_modes, cos_table, sine_table)
        block = jnp.stack([grad_real, grad_imag, coverage_patch])
        before = lax.dynamic_slice(object_sum, (anchor, row_start, col_start), (3, PATCH, PATCH))
        object_sum = lax.dynamic_update_slice(object_sum, before + block, (anchor, row_start, col_start))
        probe_sum = probe_sum + jnp.stack([pgrad_real, pgrad_imag])
        return (object_sum, probe_sum, patch_power + power)
    start = (jnp.zeros((3, NY, W), jnp.float32), jnp.zeros((2, MODES, PATCH, PATCH), jnp.float32), jnp.zeros((PATCH, PATCH), jnp.float32))
    object_sum, probe_sum, patch_power = lax.fori_loop(0, POSITIONS, visit, start)
    object_step = object_sum[:2] / (1.0 + object_sum[2])
    probe_step = probe_sum / jnp.sqrt(1.0 + patch_power)
    return (object_step, probe_step)
```

```python
import math

import jax
import jax.numpy as jnp
import numpy as np
from jax import lax
from jax.experimental import pallas as pl
from jax.experimental.pallas import tpu as pltpu
from jax.sharding import PartitionSpec as P

F32 = jnp.float32
BF16 = jnp.bfloat16
LANES = 128
SUBLANES = 8
EVEN_OFFSETS = (0, 1, 2, -2, -1, 3, -3)
ODD_OFFSETS = (0, -1, 2, -2, 1, -3, 3)
SLOTS = 7
REACH_CHIPS = 3
BITS = 4


def tables(size):
    steps = np.arange(size)
    phase = (steps[:, None] * steps[None, :] % size) * (2.0 * math.pi / size)
    factor = 1.0 / math.sqrt(size)
    cos_table, sine_table = np.cos(phase) * factor, np.sin(phase) * factor
    minus = np.block([[cos_table, -sine_table], [sine_table, cos_table]])
    plus = np.block([[cos_table, sine_table], [-sine_table, cos_table]])
    return jnp.asarray(minus, BF16), jnp.asarray(plus, BF16)


def move(value, pairs):
    return lax.ppermute(value, "tile", pairs)


def swap_bit(value, bit):
    count = lax.axis_size("tile")
    return move(value, [(i, i ^ bit) for i in range(count)])


def shift(value, steps, parities=(0, 1)):
    count = lax.axis_size("tile")
    return move(
        value,
        [(i, i + steps) for i in range(count) if (i // 2) % 2 in parities and 0 <= i + steps < count],
    )


def shift_pair(value, even_steps):
    count = lax.axis_size("tile")
    pairs = []
    for i in range(count):
        to = i + (even_steps if (i // 2) % 2 == 0 else -even_steps)
        if 0 <= to < count:
            pairs.append((i, to))
    return move(value, pairs)


def place(row, col, first_row, tile_rows, window_tiles, patch, width):
    block_tiles = (patch + tile_rows - 1) // tile_rows + 1
    local_row = row - first_row
    tile = jnp.clip(local_row // tile_rows, 0, window_tiles - block_tiles)
    col_block = jnp.minimum(col // LANES, (width - patch - LANES) // LANES)
    return tile, local_row - tile * tile_rows, pl.multiple_of(col_block * LANES, LANES), col - col_block * LANES


def positions_kernel(
    tile_rows, pos_ref, where_ref, win_ref, probe_ref, meas_ref, minus_ref, plus_ref,
    mine_ref, other_ref, psum_ref,
    raw, obj, ex, half, far, acc, grad, pacc,
):
    per_holder = meas_ref.shape[0]
    modes = probe_ref.shape[1]
    patch = probe_ref.shape[2]
    width = win_ref.shape[2]
    window_tiles = win_ref.shape[0]
    block_tiles = (patch + tile_rows - 1) // tile_rows + 1
    block_cols = patch + LANES
    first_row = where_ref[window_tiles]
    device = where_ref[window_tiles + 1]

    def clear(t, carry):
        acc[t] = jnp.zeros(acc.shape[1:], F32)
        return carry

    lax.fori_loop(0, window_tiles, clear, 0)
    pacc[...] = jnp.zeros(pacc.shape, F32)

    def visit(p, carry):
        tile, off, col, lane = place(
            pos_ref[2 * p], pos_ref[2 * p + 1], first_row, tile_rows, window_tiles, patch, width
        )
        sub = lax.rem(off, SUBLANES)
        for j in range(block_tiles):
            block = win_ref[where_ref[tile + j], :, pl.ds(col, block_cols)].astype(F32)
            raw[0, j * tile_rows : (j + 1) * tile_rows] = block[:tile_rows]
            raw[1, j * tile_rows : (j + 1) * tile_rows] = block[tile_rows:]
        for c in range(2):
            rows = raw[c, pl.ds(pl.multiple_of(off - sub, SUBLANES), patch + SUBLANES), :]
            rows = pltpu.roll(rows, lax.rem(patch + SUBLANES - sub, patch + SUBLANES), 0)[:patch]
            obj[c] = pltpu.roll(rows, lax.rem(block_cols - lane, block_cols), 1)[:, :patch]
        obj_real, obj_imag = obj[0], obj[1]
        pacc[2 * modes] = pacc[2 * modes] + (obj_real * obj_real + obj_imag * obj_imag)
        model = jnp.ones((patch, patch), F32)
        for m in range(modes):
            probe_real, probe_imag = probe_ref[0, m], probe_ref[1, m]
            ex[m, :, :patch] = (probe_real * obj[0] - probe_imag * obj[1]).astype(BF16)
            ex[m, :, patch:] = (probe_real * obj[1] + probe_imag * obj[0]).astype(BF16)
        for m in range(modes):
            out = jnp.dot(ex[m], minus_ref[...], preferred_element_type=F32).astype(BF16)
            half[m, :patch] = out[:, :patch]
            half[m, patch:] = out[:, patch:]
        for m in range(modes):
            out = jnp.dot(plus_ref[...], half[m], preferred_element_type=F32)
            far[m] = out
            model = model + (out[:patch] * out[:patch] + out[patch:] * out[patch:])
        factor = jnp.sqrt(meas_ref[p] / model) - 1.0
        for m in range(modes):
            ex[m, :, :patch] = (far[m, :patch] * factor).astype(BF16)
            ex[m, :, patch:] = (far[m, patch:] * factor).astype(BF16)
        for m in range(modes):
            out = jnp.dot(ex[m], plus_ref[...], preferred_element_type=F32).astype(BF16)
            half[m, :patch] = out[:, :patch]
            half[m, patch:] = out[:, patch:]
        grad_real = jnp.zeros((patch, patch), F32)
        grad_imag = jnp.zeros((patch, patch), F32)
        for m in range(modes):
            out = jnp.dot(minus_ref[...], half[m], preferred_element_type=F32)
            change_real, change_imag = out[:patch], out[patch:]
            probe_real, probe_imag = probe_ref[0, m], probe_ref[1, m]
            grad_real = grad_real + (probe_real * change_real + probe_imag * change_imag)
            grad_imag = grad_imag + (probe_real * change_imag - probe_imag * change_real)
            pacc[m] = pacc[m] + (obj[0] * change_real + obj[1] * change_imag)
            pacc[modes + m] = pacc[modes + m] + (obj[0] * change_imag - obj[1] * change_real)
        for c, value in enumerate((grad_real, grad_imag)):
            grad[c] = jnp.zeros(grad.shape[1:], F32)
            wide = pltpu.roll(jnp.concatenate([value, jnp.zeros((patch, LANES), F32)], axis=1), lane, 1)
            tall = jnp.concatenate([wide, jnp.zeros((SUBLANES, block_cols), F32)], axis=0)
            grad[c, pl.ds(pl.multiple_of(off - sub, SUBLANES), patch + SUBLANES), :] = pltpu.roll(tall, sub, 0)
        for j in range(block_tiles):
            at = where_ref[tile + j]
            rows = slice(j * tile_rows, (j + 1) * tile_rows)
            cols = pl.ds(col, block_cols)
            acc[at, :tile_rows, cols] = acc[at, :tile_rows, cols] + grad[0, rows]
            acc[at, tile_rows:, cols] = acc[at, tile_rows:, cols] + grad[1, rows]
        return carry

    lax.fori_loop(0, per_holder, visit, 0)

    def hand_out(t, carry):
        mine_ref[t] = acc[t].astype(BF16)
        other_ref[t] = acc[SLOTS + t].astype(BF16)
        return carry

    lax.fori_loop(0, SLOTS, hand_out, 0)
    pieces = psum_ref.shape[0]
    rows = patch // pieces

    def hand_out_probe(s, carry):
        away = sum(((s >> (BITS - 1 - b)) & 1) << b for b in range(BITS))
        piece = (device & (pieces - 1)) ^ away
        psum_ref[s] = pacc[:, pl.ds(pl.multiple_of(piece * rows, rows), rows), :].astype(BF16)
        return carry

    lax.fori_loop(0, pieces, hand_out_probe, 0)


def coverage_kernel(tile_rows, per_holder, reach, pos_ref, index_ref, probe_ref, out_ref, padded):
    modes, patch = probe_ref.shape[1], probe_ref.shape[2]
    width = out_ref.shape[1]
    block_cols = patch + LANES
    me, count = index_ref[0], index_ref[1]
    total = jnp.zeros((patch, patch), F32)
    for m in range(modes):
        total = total + (probe_ref[0, m] * probe_ref[0, m] + probe_ref[1, m] * probe_ref[1, m])
    padded[...] = jnp.zeros(padded.shape, F32)
    padded[tile_rows : tile_rows + patch] = total
    out_ref[...] = jnp.ones(out_ref.shape, F32)
    first = jnp.maximum(me - reach, 0) * per_holder
    last = (jnp.minimum(me + reach, count - 1) + 1) * per_holder

    def visit(p, carry):
        row, col = pos_ref[2 * p], pos_ref[2 * p + 1]
        at = me * tile_rows - row + tile_rows
        col_block = jnp.minimum(col // LANES, (width - patch - LANES) // LANES)
        cols = pl.ds(pl.multiple_of(col_block * LANES, LANES), block_cols)

        @pl.when(jnp.logical_and(at > 0, at < tile_rows + patch))
        def _():
            sub = lax.rem(at, SUBLANES)
            rows = padded[pl.ds(pl.multiple_of(at - sub, SUBLANES), tile_rows + SUBLANES), :]
            rows = pltpu.roll(rows, lax.rem(tile_rows + SUBLANES - sub, tile_rows + SUBLANES), 0)[:tile_rows]
            wide = jnp.concatenate([rows, jnp.zeros((tile_rows, LANES), F32)], axis=1)
            out_ref[:, cols] = out_ref[:, cols] + pltpu.roll(wide, col - col_block * LANES, 1)

        return carry

    lax.fori_loop(first, last, visit, 0)


def unpack_kernel(index_ref, pieces_ref, out_ref):
    pieces, planes, rows, cols = pieces_ref.shape
    modes = out_ref.shape[1]
    device = index_ref[0]

    def visit(s, carry):
        away = sum(((s >> (BITS - 1 - b)) & 1) << b for b in range(BITS))
        piece = (device & (pieces - 1)) ^ away
        at = pl.ds(pl.multiple_of(piece * rows, rows), rows)
        value = pieces_ref[s].astype(F32)
        for c in range(2):
            out_ref[c, :, at, :] = value[c * modes : (c + 1) * modes]
        return carry

    lax.fori_loop(0, pieces, visit, 0)


VMEM = pl.BlockSpec(memory_space=pltpu.VMEM)
SMEM = pl.BlockSpec(memory_space=pltpu.SMEM)


def add(a, b):
    return (a.astype(F32) + b.astype(F32)).astype(BF16)


def local(object_field, probe_modes, positions, intensity):
    tile_rows, width = object_field.shape[1:]
    modes, patch = probe_modes.shape[1:3]
    per_holder = positions.shape[0]
    reach = (patch - 1) // tile_rows
    count = lax.axis_size("tile")
    me = lax.axis_index("tile")
    core, chip = me % 2, me // 2
    even = chip % 2 == 0
    block_tiles = (patch + tile_rows - 1) // tile_rows + 1
    block_cols = patch + LANES
    tiles = 2 * SLOTS

    everyone = lax.all_gather(positions, "tile").reshape(-1)

    own = object_field.astype(BF16).reshape(2 * tile_rows, width)
    from_y = swap_bit(own, 2)
    from_up = shift(own, -4)
    from_down = shift(own, 4)
    from_t = swap_bit(jnp.where(even, from_up, from_down), 2)
    from_s = shift_pair(from_y, -4)
    from_r = shift_pair(from_t, 4)
    mine = [own, from_y, from_up, from_down, from_t, from_s, from_r]
    window = jnp.stack(mine + [swap_bit(v, 1) for v in mine])

    slot_of = {}
    for name, offsets in (("even", EVEN_OFFSETS), ("odd", ODD_OFFSETS)):
        slot_of[name] = np.array([offsets.index(w // 2 - REACH_CHIPS) for w in range(tiles)])
    slot = jnp.where(even, slot_of["even"], slot_of["odd"])
    where = slot + SLOTS * (np.arange(tiles) % 2 != core)
    first_row = (2 * (chip - REACH_CHIPS)) * tile_rows
    where = jnp.concatenate([where, first_row[None], me[None]]).astype(jnp.int32)

    minus, plus = tables(patch)
    pieces = 2**BITS
    rows = patch // pieces
    planes = 2 * modes + 1
    mine, other, psum = pl.pallas_call(
        lambda *refs: positions_kernel(tile_rows, *refs),
        out_shape=(
            jax.ShapeDtypeStruct((SLOTS, 2 * tile_rows, width), BF16),
            jax.ShapeDtypeStruct((SLOTS, 2 * tile_rows, width), BF16),
            jax.ShapeDtypeStruct((pieces, planes, rows, patch), BF16),
        ),
        in_specs=[SMEM, SMEM, VMEM, VMEM, VMEM, VMEM, VMEM],
        out_specs=(VMEM, VMEM, VMEM),
        scratch_shapes=[
            pltpu.VMEM((2, block_tiles * tile_rows + 16, block_cols), F32),
            pltpu.VMEM((2, patch, patch), F32),
            pltpu.VMEM((modes, patch, 2 * patch), BF16),
            pltpu.VMEM((modes, 2 * patch, patch), BF16),
            pltpu.VMEM((modes, 2 * patch, patch), F32),
            pltpu.VMEM((tiles, 2 * tile_rows, width), F32),
            pltpu.VMEM((2, block_tiles * tile_rows + 16, block_cols), F32),
            pltpu.VMEM((planes, patch, patch), F32),
        ],
        compiler_params=pltpu.CompilerParams(vmem_limit_bytes=48 * 1024 * 1024),
        cost_estimate=pl.CostEstimate(flops=10_000_000_000, bytes_accessed=20_000_000, transcendentals=0),
        name="positions",
    )(positions.reshape(-1), where, window, probe_modes, intensity, minus, plus)

    psum = psum.reshape((2,) * BITS + (planes, rows, patch))
    for bit in range(BITS):
        psum = add(psum[0], swap_bit(psum[1], 1 << bit))
    bit = 1 << BITS
    while bit < count:
        psum = add(psum, swap_bit(psum, bit))
        bit *= 2
    psum = psum.astype(F32)
    pstep = (psum[: 2 * modes] / jnp.sqrt(1.0 + psum[2 * modes])).astype(BF16)
    for bit in reversed(range(BITS)):
        pstep = jnp.stack([pstep, swap_bit(pstep, 1 << bit)])
    pstep = pstep.reshape(pieces, 2 * modes, rows, patch)
    probe_step = pl.pallas_call(
        unpack_kernel,
        out_shape=jax.ShapeDtypeStruct(probe_modes.shape, F32),
        in_specs=[SMEM, VMEM],
        out_specs=VMEM,
        compiler_params=pltpu.CompilerParams(vmem_limit_bytes=16 * 1024 * 1024),
        cost_estimate=pl.CostEstimate(flops=1_000_000, bytes_accessed=3_000_000, transcendentals=0),
        name="probe_unpack",
    )(me[None].astype(jnp.int32), pstep)

    own_sum, y_sum, up_sum, down_sum, t_sum, s_sum, r_sum = [
        add(mine[j], swap_bit(other[j], 1)) for j in range(SLOTS)
    ]
    t_sum = add(t_sum, shift_pair(r_sum, -4))
    y_sum = add(y_sum, shift_pair(s_sum, 4))
    t_came = swap_bit(t_sum, 2)
    up_sum = add(up_sum, jnp.where(even, t_came, 0))
    down_sum = add(down_sum, jnp.where(even, 0, t_came))
    y_came = swap_bit(y_sum, 2)
    from_below = shift(up_sum, 4)
    from_above = shift(down_sum, -4)
    total = (
        own_sum.astype(F32) + y_came.astype(F32) + from_below.astype(F32) + from_above.astype(F32)
    ).reshape(2, tile_rows, width)

    coverage = pl.pallas_call(
        lambda *refs: coverage_kernel(tile_rows, per_holder, reach, *refs),
        out_shape=jax.ShapeDtypeStruct((tile_rows, width), F32),
        in_specs=[SMEM, SMEM, VMEM],
        out_specs=VMEM,
        scratch_shapes=[pltpu.VMEM((patch + 2 * tile_rows + 16, patch), F32)],
        compiler_params=pltpu.CompilerParams(vmem_limit_bytes=16 * 1024 * 1024),
        cost_estimate=pl.CostEstimate(flops=10_000_000, bytes_accessed=3_000_000, transcendentals=0),
        name="coverage",
    )(everyone, jnp.stack([me, count]).astype(jnp.int32), probe_modes)
    return (total / coverage[None], probe_step)


def solution(mesh):
    in_specs = (
        P(None, ("grp", "tile"), None),
        P(None, "grp", None, None),
        P(("grp", "tile"), None),
        P(("grp", "tile"), None, None),
    )
    out_specs = (P(None, ("grp", "tile"), None), P(None, "grp", None, None))
    return jax.shard_map(local, mesh=mesh, in_specs=in_specs, out_specs=out_specs, check_vma=False)
```

```python
import math

import jax
import jax.numpy as jnp
import numpy as np
from jax import lax
from jax.experimental import pallas as pl
from jax.experimental.pallas import tpu as pltpu
from jax.sharding import PartitionSpec as P

F32 = jnp.float32
BF16 = jnp.bfloat16
LANES = 128
SUBLANES = 8
MIB = 1024 * 1024
EVEN_OFFSETS = (0, 1, 2, -2, -1, 3, -3)
SLOTS = 7
REACH_CHIPS = 3
BITS = 4
HEAD_ROWS = 16
BASE = 128


def real_tables(size):
    steps = np.arange(size)
    phase = (steps[:, None] * steps[None, :] % size) * (2.0 * math.pi / size)
    factor = 1.0 / math.sqrt(size)
    cos_table, sine_table = np.cos(phase) * factor, np.sin(phase) * factor
    mid = size // 2
    table = np.concatenate([cos_table[:, :mid], cos_table[:, mid : mid + 1], sine_table[:, 1:mid]], axis=1)
    return jnp.asarray(table, BF16), jnp.asarray(table.T.copy(), BF16)


def frequency_order(size):
    mid = size // 2
    order = np.concatenate([np.arange(mid), [mid], np.arange(size - 1, mid, -1)])
    return np.eye(size, dtype=np.float32)[order]


def dot(a, b):
    return jnp.dot(a, b, preferred_element_type=F32)


def with_first_row(first, rest):
    row = lax.broadcasted_iota(jnp.int32, (SUBLANES, rest.shape[1]), 0)
    top = jnp.where(row == 0, first[:SUBLANES], rest[:SUBLANES])
    return jnp.concatenate([top, rest[SUBLANES:]], axis=0)


def with_first_lane(first, rest):
    lane = lax.broadcasted_iota(jnp.int32, rest.shape, 1)
    return jnp.where(lane == 0, first, rest)


def unfold(pick, axis, u, v):
    mid = u.shape[axis] // 2
    part = (lambda x, i: x[i * mid : (i + 1) * mid]) if axis == 0 else (lambda x, i: x[:, i * mid : (i + 1) * mid])
    u1, u2, v1, v2 = part(u, 0), part(u, 1), part(v, 0), part(v, 1)
    real = jnp.concatenate([pick(u1, u1 + v2), pick(u2, u1 - v2)], axis=axis)
    imag = jnp.concatenate([pick(v1, v1 - u2), pick(v2, v1 + u2)], axis=axis)
    return real, imag


def fold(pick, axis, real, imag):
    mid = real.shape[axis] // 2
    part = (lambda x, i: x[i * mid : (i + 1) * mid]) if axis == 0 else (lambda x, i: x[:, i * mid : (i + 1) * mid])
    r1, r2, i1, i2 = part(real, 0), part(real, 1), part(imag, 0), part(imag, 1)
    a = jnp.concatenate([pick(r1, r1 + r2), pick(r2, i2 - i1)], axis=axis)
    b = jnp.concatenate([pick(i1, i1 + i2), pick(i2, r1 - r2)], axis=axis)
    return a.astype(BF16), b.astype(BF16)


def positions_kernel(
    tile_rows, pos_ref, where_ref, win_ref, probe_ref, meas_ref, right_ref, left_ref, *rest
):
    slots = win_ref.shape[0]
    out_refs, psum_ref = rest[:slots], rest[slots]
    raw, obj, far, sums, grad, pacc = rest[slots + 1 :]
    per_holder = meas_ref.shape[0]
    modes = probe_ref.shape[1]
    patch = probe_ref.shape[2]
    both = 2 * tile_rows
    width = sums.shape[2]
    block_tiles = (patch + tile_rows - 1) // tile_rows + 1
    block_rows = block_tiles * tile_rows
    first_row = where_ref[slots]
    device = where_ref[slots + 1]
    tall = patch // SUBLANES
    sublane = lax.broadcasted_iota(jnp.int32, (tall + 1, SUBLANES, LANES), 1)
    lanes = lax.broadcasted_iota(jnp.int32, (patch, LANES), 1)
    cols = patch // LANES

    def clear(t, carry):
        sums[t] = jnp.zeros(sums.shape[1:], BF16)
        return carry

    lax.fori_loop(0, slots, clear, 0)
    pacc[...] = jnp.zeros(pacc.shape, F32)

    def visit(p, carry):
        tile, off, block, lane = place(
            pos_ref[2 * p], pos_ref[2 * p + 1], first_row, tile_rows, slots, patch, width
        )
        sub = lax.rem(off, SUBLANES)
        base = pl.multiple_of(off - sub, SUBLANES)
        for j in range(block_tiles):
            for q in range(cols + 1):
                at = pl.ds(pl.multiple_of((block + q) * both, 16), both)
                part = win_ref[where_ref[tile + j], at, :].astype(F32)
                raw[0, q, j * tile_rows : (j + 1) * tile_rows] = part[:tile_rows]
                raw[1, q, j * tile_rows : (j + 1) * tile_rows] = part[tile_rows:]
        for c in range(2):
            turned = []
            for q in range(cols + 1):
                rows = raw[c, q, pl.ds(base, patch + SUBLANES), :].reshape(tall + 1, SUBLANES, LANES)
                rows = pltpu.roll(rows, lax.rem(SUBLANES - sub, SUBLANES), 1)
                rows = jnp.where(sublane[:tall] < SUBLANES - sub, rows[:tall], rows[1:])
                turned.append(pltpu.roll(rows.reshape(patch, LANES), lax.rem(LANES - lane, LANES), 1))
            for q in range(cols):
                obj[c, :, q * LANES : (q + 1) * LANES] = jnp.where(lanes < LANES - lane, turned[q], turned[q + 1])
        pacc[2 * modes] = pacc[2 * modes] + (obj[0] * obj[0] + obj[1] * obj[1])
        model = jnp.ones((patch, patch), F32)
        for m in range(modes):
            probe_real, probe_imag = probe_ref[0, m], probe_ref[1, m]
            exit_real = (probe_real * obj[0] - probe_imag * obj[1]).astype(BF16)
            exit_imag = (probe_real * obj[1] + probe_imag * obj[0]).astype(BF16)
            half_real, half_imag = unfold(
                with_first_lane, 1, dot(exit_real, right_ref[...]), dot(exit_imag, right_ref[...])
            )
            far_real, far_imag = unfold(
                with_first_row, 0, dot(left_ref[...], half_real.astype(BF16)), dot(left_ref[...], half_imag.astype(BF16))
            )
            far[0, m] = far_real
            far[1, m] = far_imag
            model = model + (far_real * far_real + far_imag * far_imag)
        factor = jnp.sqrt(meas_ref[p] / model) - 1.0
        grad_real = jnp.zeros((patch, patch), F32)
        grad_imag = jnp.zeros((patch, patch), F32)
        for m in range(modes):
            a, b = fold(with_first_lane, 1, far[0, m] * factor, far[1, m] * factor)
            a, b = fold(with_first_row, 0, dot(a, left_ref[...]), dot(b, left_ref[...]))
            change_real, change_imag = dot(right_ref[...], a), dot(right_ref[...], b)
            probe_real, probe_imag = probe_ref[0, m], probe_ref[1, m]
            grad_real = grad_real + (probe_real * change_real + probe_imag * change_imag)
            grad_imag = grad_imag + (probe_real * change_imag - probe_imag * change_real)
            pacc[m] = pacc[m] + (obj[0] * change_real + obj[1] * change_imag)
            pacc[modes + m] = pacc[modes + m] + (obj[0] * change_imag - obj[1] * change_real)
        edge = jnp.zeros((1, SUBLANES, LANES), F32)
        for c, value in enumerate((grad_real, grad_imag)):
            turned = [
                pltpu.roll(value[:, q * LANES : (q + 1) * LANES], lax.rem(lane, LANES), 1) for q in range(cols)
            ]
            for q in range(cols + 1):
                here = turned[q] if q < cols else jnp.zeros((patch, LANES), F32)
                before = turned[q - 1] if q > 0 else jnp.zeros((patch, LANES), F32)
                wide = jnp.where(lanes >= lane, here, before).reshape(tall, SUBLANES, LANES)
                wide = pltpu.roll(wide, sub, 1)
                wide = jnp.where(
                    sublane >= sub, jnp.concatenate([wide, edge], axis=0), jnp.concatenate([edge, wide], axis=0)
                )
                grad[c, q] = jnp.zeros(grad.shape[2:], F32)
                grad[c, q, pl.ds(base, patch + SUBLANES), :] = wide.reshape(patch + SUBLANES, LANES)
        for j in range(block_tiles):
            slot = where_ref[tile + j]
            rows = slice(j * tile_rows, (j + 1) * tile_rows)
            for q in range(cols + 1):
                at = pl.ds(pl.multiple_of((block + q) * LANES, LANES), LANES)
                part = jnp.concatenate([grad[0, q, rows], grad[1, q, rows]], axis=0)
                sums[slot, :, at] = (sums[slot, :, at].astype(F32) + part).astype(BF16)
        return carry

    lax.fori_loop(0, per_holder, visit, 0)

    for t in range(slots):
        out_refs[t][...] = sums[t]
    pieces = psum_ref.shape[0]
    rows = patch // pieces

    def hand_out_probe(s, carry):
        away = sum(((s >> (BITS - 1 - b)) & 1) << b for b in range(BITS))
        piece = (device & (pieces - 1)) ^ away
        psum_ref[s] = pacc[:, pl.ds(pl.multiple_of(piece * rows, rows), rows), :].astype(BF16)
        return carry

    lax.fori_loop(0, pieces, hand_out_probe, 0)

def move(value, pairs):
    return lax.ppermute(value, "tile", pairs)


def swap_bit(value, bit):
    count = lax.axis_size("tile")
    return move(value, [(i, i ^ bit) for i in range(count)])


def shift_pair(value, even_steps):
    count = lax.axis_size("tile")
    pairs = []
    for i in range(count):
        to = i + (even_steps if (i // 2) % 2 == 0 else -even_steps)
        if 0 <= to < count:
            pairs.append((i, to))
    return move(value, pairs)


def place(row, col, first_row, tile_rows, window_tiles, patch, width):
    block_tiles = (patch + tile_rows - 1) // tile_rows + 1
    local_row = row - first_row
    tile = jnp.clip(local_row // tile_rows, 0, window_tiles - block_tiles)
    block = jnp.minimum(col // LANES, (width - patch - LANES) // LANES)
    return tile, local_row - tile * tile_rows, block, col - block * LANES


def pack_kernel(pos_ref, obj_ref, out_ref):
    tile_rows, width = obj_ref.shape[1:]
    both = 2 * tile_rows
    for q in range(width // LANES):
        part = obj_ref[:, :, q * LANES : (q + 1) * LANES].reshape(both, LANES)
        out_ref[q * both : (q + 1) * both] = part.astype(BF16)
    lane = lax.broadcasted_iota(jnp.int32, (HEAD_ROWS, LANES), 1)
    head = jnp.zeros((HEAD_ROWS, LANES), jnp.int32)
    for k in range(pos_ref.shape[0]):
        value = pos_ref[k]
        head = jnp.where(lane == 2 * k, value // BASE, head)
        head = jnp.where(lane == 2 * k + 1, lax.rem(value, BASE), head)
    out_ref[width // LANES * both :] = head.astype(F32).astype(BF16)


def coverage_kernel(tile_rows, per_holder, index_ref, heads_ref, probe_ref, out_ref, padded, digits, pos_ref):
    modes, patch = probe_ref.shape[1], probe_ref.shape[2]
    width = out_ref.shape[1]
    slots = heads_ref.shape[0]
    block_cols = patch + LANES
    me, count = index_ref[slots], index_ref[slots + 1]
    heads = heads_ref[...].astype(F32)
    for s in range(slots):
        row = heads[s, :SUBLANES]
        digits[s] = (row * BASE + pltpu.roll(row, LANES - 1, 1)).astype(jnp.int32)
    pltpu.sync_copy(digits, pos_ref)
    total = jnp.zeros((patch, patch), F32)
    for m in range(modes):
        total = total + (probe_ref[0, m] * probe_ref[0, m] + probe_ref[1, m] * probe_ref[1, m])
    padded[...] = jnp.zeros(padded.shape, F32)
    padded[tile_rows : tile_rows + patch] = total
    out_ref[...] = jnp.ones(out_ref.shape, F32)

    def visit(k, carry):
        s, p = k // per_holder, lax.rem(k, per_holder)
        holder = index_ref[s]
        row, col = pos_ref[s, 0, 4 * p], pos_ref[s, 0, 4 * p + 2]
        at = me * tile_rows - row + tile_rows
        col_block = jnp.minimum(col // LANES, (width - patch - LANES) // LANES)
        cols = pl.ds(pl.multiple_of(col_block * LANES, LANES), block_cols)
        there = jnp.logical_and(holder >= 0, holder < count)

        @pl.when(jnp.logical_and(there, jnp.logical_and(at > 0, at < tile_rows + patch)))
        def _():
            sub = lax.rem(at, SUBLANES)
            rows = padded[pl.ds(pl.multiple_of(at - sub, SUBLANES), tile_rows + SUBLANES), :]
            rows = pltpu.roll(rows, lax.rem(tile_rows + SUBLANES - sub, tile_rows + SUBLANES), 0)[:tile_rows]
            wide = jnp.concatenate([rows, jnp.zeros((tile_rows, LANES), F32)], axis=1)
            out_ref[:, cols] = out_ref[:, cols] + pltpu.roll(wide, col - col_block * LANES, 1)

        return carry

    lax.fori_loop(0, slots * per_holder, visit, 0)


def order_kernel(order_ref, meas_ref, out_ref):
    turn = order_ref[...]
    for p in range(meas_ref.shape[0]):
        rows = jnp.dot(turn, meas_ref[p], preferred_element_type=F32, precision=lax.Precision.HIGHEST)
        out_ref[p] = lax.dot_general(
            rows, turn, (((1,), (1,)), ((), ())), preferred_element_type=F32, precision=lax.Precision.HIGHEST
        )


def unpack_kernel(index_ref, pieces_ref, out_ref):
    pieces, planes, rows, cols = pieces_ref.shape
    modes = out_ref.shape[1]
    device = index_ref[0]

    def visit(s, carry):
        away = sum(((s >> (BITS - 1 - b)) & 1) << b for b in range(BITS))
        piece = (device & (pieces - 1)) ^ away
        at = pl.ds(pl.multiple_of(piece * rows, rows), rows)
        value = pieces_ref[s].astype(F32)
        for c in range(2):
            out_ref[c, :, at, :] = value[c * modes : (c + 1) * modes]
        return carry

    lax.fori_loop(0, pieces, visit, 0)


VMEM = pl.BlockSpec(memory_space=pltpu.VMEM)
SMEM = pl.BlockSpec(memory_space=pltpu.SMEM)


def call(kernel, name, out_shape, in_specs, limit, flops, bytes_accessed, scratch=()):
    return pl.pallas_call(
        kernel,
        out_shape=out_shape,
        in_specs=in_specs,
        out_specs=jax.tree.map(lambda _: VMEM, out_shape),
        scratch_shapes=list(scratch),
        compiler_params=pltpu.CompilerParams(vmem_limit_bytes=limit * MIB),
        cost_estimate=pl.CostEstimate(flops=flops, bytes_accessed=bytes_accessed, transcendentals=0),
        name=name,
    )


def add(a, b):
    return (a.astype(F32) + b.astype(F32)).astype(BF16)


def local(object_field, probe_modes, positions, intensity):
    tile_rows, width = object_field.shape[1:]
    modes, patch = probe_modes.shape[1:3]
    per_holder = positions.shape[0]
    count = lax.axis_size("tile")
    me = lax.axis_index("tile")
    core, chip = me % 2, me // 2
    block_rows = ((patch + tile_rows - 1) // tile_rows + 1) * tile_rows
    both = 2 * tile_rows
    tiles = 2 * SLOTS
    mine_first = positions.reshape(-1)

    own = call(
        pack_kernel, "pack", jax.ShapeDtypeStruct((width // LANES * both + HEAD_ROWS, LANES), BF16), [SMEM, VMEM],
        8, 1_000_000, 1_000_000,
    )(mine_first, object_field)
    from_m = shift_pair(own, -4)
    from_y = swap_bit(own, 2)
    from_n = shift_pair(own, 4)
    from_t = swap_bit(from_m, 2)
    from_s = shift_pair(from_y, -4)
    from_r = shift_pair(from_t, 4)
    mine = [own, from_y, from_m, from_n, from_t, from_s, from_r]
    window = jnp.stack(mine + [swap_bit(v, 1) for v in mine])

    offsets = np.array(EVEN_OFFSETS)
    slot_of = np.array([EVEN_OFFSETS.index(w // 2 - REACH_CHIPS) for w in range(tiles)])
    back_slot_of = np.array([EVEN_OFFSETS.index(REACH_CHIPS - w // 2) for w in range(tiles)])
    even = chip % 2 == 0
    chips = chip + jnp.where(even, offsets, -offsets)
    holders = jnp.concatenate([2 * chips + core, 2 * chips + 1 - core])
    index = jnp.concatenate([holders, me[None], jnp.full((1,), count)]).astype(jnp.int32)
    where = jnp.where(even, slot_of, back_slot_of) + SLOTS * (np.arange(tiles) % 2 != core)
    first_row = (2 * (chip - REACH_CHIPS)) * tile_rows
    where = jnp.concatenate([where, first_row[None], me[None]]).astype(jnp.int32)

    coverage = call(
        lambda *refs: coverage_kernel(tile_rows, per_holder, *refs), "coverage",
        jax.ShapeDtypeStruct((tile_rows, width), F32), [SMEM, VMEM, VMEM],
        8, 10_000_000, 3_000_000,
        [
            pltpu.VMEM((patch + 2 * tile_rows + 16, patch), F32),
            pltpu.VMEM((tiles, SUBLANES, LANES), jnp.int32),
            pltpu.SMEM((tiles, SUBLANES, LANES), jnp.int32),
        ],
    )(index, window[:, -HEAD_ROWS:], probe_modes)

    right, left = real_tables(patch)
    ordered = call(
        order_kernel, "order", jax.ShapeDtypeStruct(intensity.shape, F32), [VMEM, VMEM], 8, 2_000_000_000, 2_000_000
    )(jnp.asarray(frequency_order(patch)), intensity)

    pieces = 2**BITS
    rows = patch // pieces
    planes = 2 * modes + 1
    cols = patch // LANES
    *sums, psum = call(
        lambda *refs: positions_kernel(tile_rows, *refs), "positions",
        (jax.ShapeDtypeStruct((both, width), BF16),) * tiles + (jax.ShapeDtypeStruct((pieces, planes, rows, patch), BF16),),
        [SMEM, SMEM, VMEM, VMEM, VMEM, VMEM, VMEM],
        24, 10_000_000_000, 20_000_000,
        [
            pltpu.VMEM((2, cols + 1, block_rows + 16, LANES), F32),
            pltpu.VMEM((2, patch, patch), F32),
            pltpu.VMEM((2, modes, patch, patch), F32),
            pltpu.VMEM((tiles, both, width), BF16),
            pltpu.VMEM((2, cols + 1, block_rows + 16, LANES), F32),
            pltpu.VMEM((planes, patch, patch), F32),
        ],
    )(mine_first, where, window, probe_modes, ordered, right, left)

    psum = psum.reshape((2,) * BITS + (planes, rows, patch))
    for bit in range(BITS):
        psum = add(psum[0], swap_bit(psum[1], 1 << bit))
    bit = 1 << BITS
    while bit < count:
        psum = add(psum, swap_bit(psum, bit))
        bit *= 2
    psum = psum.astype(F32)
    pstep = (psum[: 2 * modes] / jnp.sqrt(1.0 + psum[2 * modes])).astype(BF16)
    for bit in reversed(range(BITS)):
        pstep = jnp.stack([pstep, swap_bit(pstep, 1 << bit)])
    pstep = pstep.reshape(pieces, 2 * modes, rows, patch)
    probe_step = call(
        unpack_kernel, "probe_unpack", jax.ShapeDtypeStruct(probe_modes.shape, F32), [SMEM, VMEM], 8, 1_000_000, 3_000_000
    )(me[None].astype(jnp.int32), pstep)

    own_sum, y_sum, m_sum, n_sum, t_sum, s_sum, r_sum = [add(sums[j], swap_bit(sums[SLOTS + j], 1)) for j in range(SLOTS)]
    t_sum = add(t_sum, shift_pair(r_sum, -4))
    y_sum = add(y_sum, shift_pair(s_sum, 4))
    n_came = shift_pair(n_sum, -4)
    m_sum = add(m_sum, swap_bit(t_sum, 2))
    y_came = swap_bit(y_sum, 2)
    m_came = shift_pair(m_sum, 4)
    total = own_sum.astype(F32) + y_came.astype(F32) + m_came.astype(F32) + n_came.astype(F32)
    return (total.reshape(2, tile_rows, width) / coverage[None], probe_step)


def solution(mesh):
    in_specs = (
        P(None, ("grp", "tile"), None),
        P(None, "grp", None, None),
        P(("grp", "tile"), None),
        P(("grp", "tile"), None, None),
    )
    out_specs = (P(None, ("grp", "tile"), None), P(None, "grp", None, None))
    return jax.shard_map(local, mesh=mesh, in_specs=in_specs, out_specs=out_specs, check_vma=False)
```

```python
import math

import jax
import jax.numpy as jnp
import numpy as np
from jax import lax
from jax.experimental import pallas as pl
from jax.experimental.pallas import tpu as pltpu
from jax.sharding import PartitionSpec as P

F32 = jnp.float32
BF16 = jnp.bfloat16
LANES = 128
SUBLANES = 8
MIB = 1024 * 1024
BROUGHT = ((2, -1, -3), (1, -2, 3))
REACH_CHIPS = 3
PROBE_BITS = ((2, 4, 8), (4, 8, 2))
BITS = 4
HEAD_ROWS = 16
BASE = 128


def real_tables(size):
    steps = np.arange(size)
    phase = (steps[:, None] * steps[None, :] % size) * (2.0 * math.pi / size)
    factor = 1.0 / math.sqrt(size)
    cos_table, sine_table = np.cos(phase) * factor, np.sin(phase) * factor
    mid = size // 2
    table = np.concatenate([cos_table[:, :mid], cos_table[:, mid : mid + 1], sine_table[:, 1:mid]], axis=1)
    return jnp.asarray(table, BF16), jnp.asarray(table.T.copy(), BF16)


def frequency_order(size):
    mid = size // 2
    order = np.concatenate([np.arange(mid), [mid], np.arange(size - 1, mid, -1)])
    return np.eye(size, dtype=np.float32)[order]


def dot(a, b):
    return jnp.dot(a, b, preferred_element_type=F32)


def with_first_row(first, rest):
    row = lax.broadcasted_iota(jnp.int32, (SUBLANES, rest.shape[1]), 0)
    top = jnp.where(row == 0, first[:SUBLANES], rest[:SUBLANES])
    return jnp.concatenate([top, rest[SUBLANES:]], axis=0)


def with_first_lane(first, rest):
    lane = lax.broadcasted_iota(jnp.int32, rest.shape, 1)
    return jnp.where(lane == 0, first, rest)


def unfold(pick, axis, u, v):
    mid = u.shape[axis] // 2
    part = (lambda x, i: x[i * mid : (i + 1) * mid]) if axis == 0 else (lambda x, i: x[:, i * mid : (i + 1) * mid])
    u1, u2, v1, v2 = part(u, 0), part(u, 1), part(v, 0), part(v, 1)
    real = jnp.concatenate([pick(u1, u1 + v2), pick(u2, u1 - v2)], axis=axis)
    imag = jnp.concatenate([pick(v1, v1 - u2), pick(v2, v1 + u2)], axis=axis)
    return real, imag


def fold(pick, axis, real, imag):
    mid = real.shape[axis] // 2
    part = (lambda x, i: x[i * mid : (i + 1) * mid]) if axis == 0 else (lambda x, i: x[:, i * mid : (i + 1) * mid])
    r1, r2, i1, i2 = part(real, 0), part(real, 1), part(imag, 0), part(imag, 1)
    a = jnp.concatenate([pick(r1, r1 + r2), pick(r2, i2 - i1)], axis=axis)
    b = jnp.concatenate([pick(i1, i1 + i2), pick(i2, r1 - r2)], axis=axis)
    return a.astype(BF16), b.astype(BF16)


def positions_kernel(
    tile_rows, pos_ref, where_ref, win_ref, probe_ref, meas_ref, right_ref, left_ref, *rest
):
    slots = win_ref.shape[0]
    *out_refs, psum_ref, raw, obj, far, sums, grad, pacc = rest
    per_holder = meas_ref.shape[0]
    modes = probe_ref.shape[1]
    patch = probe_ref.shape[2]
    both = 2 * tile_rows
    width = sums.shape[2]
    block_tiles = (patch + tile_rows - 1) // tile_rows + 1
    block_rows = block_tiles * tile_rows
    first_row = where_ref[slots]
    device = where_ref[slots + 1]
    tall = patch // SUBLANES
    sublane = lax.broadcasted_iota(jnp.int32, (tall + 1, SUBLANES, LANES), 1)
    lanes = lax.broadcasted_iota(jnp.int32, (patch, LANES), 1)
    cols = patch // LANES

    def clear(t, carry):
        sums[t] = jnp.zeros(sums.shape[1:], BF16)
        return carry

    lax.fori_loop(0, slots, clear, 0)
    pacc[...] = jnp.zeros(pacc.shape, F32)

    def visit(p, carry):
        tile, off, block, lane = place(
            pos_ref[2 * p], pos_ref[2 * p + 1], first_row, tile_rows, slots, patch, width
        )
        sub = lax.rem(off, SUBLANES)
        base = pl.multiple_of(off - sub, SUBLANES)
        for j in range(block_tiles):
            for q in range(cols + 1):
                at = pl.ds(pl.multiple_of((block + q) * both, 16), both)
                part = win_ref[where_ref[tile + j], at, :].astype(F32)
                raw[0, q, j * tile_rows : (j + 1) * tile_rows] = part[:tile_rows]
                raw[1, q, j * tile_rows : (j + 1) * tile_rows] = part[tile_rows:]
        for c in range(2):
            turned = []
            for q in range(cols + 1):
                rows = raw[c, q, pl.ds(base, patch + SUBLANES), :].reshape(tall + 1, SUBLANES, LANES)
                rows = pltpu.roll(rows, lax.rem(SUBLANES - sub, SUBLANES), 1)
                rows = jnp.where(sublane[:tall] < SUBLANES - sub, rows[:tall], rows[1:])
                turned.append(pltpu.roll(rows.reshape(patch, LANES), lax.rem(LANES - lane, LANES), 1))
            for q in range(cols):
                obj[c, :, q * LANES : (q + 1) * LANES] = jnp.where(lanes < LANES - lane, turned[q], turned[q + 1])
        pacc[2 * modes] = pacc[2 * modes] + (obj[0] * obj[0] + obj[1] * obj[1])
        model = jnp.ones((patch, patch), F32)
        for m in range(modes):
            probe_real, probe_imag = probe_ref[0, m], probe_ref[1, m]
            exit_real = (probe_real * obj[0] - probe_imag * obj[1]).astype(BF16)
            exit_imag = (probe_real * obj[1] + probe_imag * obj[0]).astype(BF16)
            half_real, half_imag = unfold(
                with_first_lane, 1, dot(exit_real, right_ref[...]), dot(exit_imag, right_ref[...])
            )
            far_real, far_imag = unfold(
                with_first_row, 0, dot(left_ref[...], half_real.astype(BF16)), dot(left_ref[...], half_imag.astype(BF16))
            )
            far[0, m] = far_real
            far[1, m] = far_imag
            model = model + (far_real * far_real + far_imag * far_imag)
        factor = jnp.sqrt(meas_ref[p] / model) - 1.0
        grad_real = jnp.zeros((patch, patch), F32)
        grad_imag = jnp.zeros((patch, patch), F32)
        for m in range(modes):
            a, b = fold(with_first_lane, 1, far[0, m] * factor, far[1, m] * factor)
            a, b = fold(with_first_row, 0, dot(a, left_ref[...]), dot(b, left_ref[...]))
            change_real, change_imag = dot(right_ref[...], a), dot(right_ref[...], b)
            probe_real, probe_imag = probe_ref[0, m], probe_ref[1, m]
            grad_real = grad_real + (probe_real * change_real + probe_imag * change_imag)
            grad_imag = grad_imag + (probe_real * change_imag - probe_imag * change_real)
            pacc[m] = pacc[m] + (obj[0] * change_real + obj[1] * change_imag)
            pacc[modes + m] = pacc[modes + m] + (obj[0] * change_imag - obj[1] * change_real)
        edge = jnp.zeros((1, SUBLANES, LANES), F32)
        for c, value in enumerate((grad_real, grad_imag)):
            turned = [
                pltpu.roll(value[:, q * LANES : (q + 1) * LANES], lax.rem(lane, LANES), 1) for q in range(cols)
            ]
            for q in range(cols + 1):
                here = turned[q] if q < cols else jnp.zeros((patch, LANES), F32)
                before = turned[q - 1] if q > 0 else jnp.zeros((patch, LANES), F32)
                wide = jnp.where(lanes >= lane, here, before).reshape(tall, SUBLANES, LANES)
                wide = pltpu.roll(wide, sub, 1)
                wide = jnp.where(
                    sublane >= sub, jnp.concatenate([wide, edge], axis=0), jnp.concatenate([edge, wide], axis=0)
                )
                grad[c, q] = jnp.zeros(grad.shape[2:], F32)
                grad[c, q, pl.ds(base, patch + SUBLANES), :] = wide.reshape(patch + SUBLANES, LANES)
        for j in range(block_tiles):
            slot = where_ref[tile + j]
            rows = slice(j * tile_rows, (j + 1) * tile_rows)
            for q in range(cols + 1):
                at = pl.ds(pl.multiple_of((block + q) * LANES, LANES), LANES)
                part = jnp.concatenate([grad[0, q, rows], grad[1, q, rows]], axis=0)
                sums[slot, :, at] = (sums[slot, :, at].astype(F32) + part).astype(BF16)
        return carry

    lax.fori_loop(0, per_holder, visit, 0)

    at = 0
    for ref in out_refs:
        for t in range(ref.shape[0] // both):
            ref[t * both : (t + 1) * both] = sums[at]
            at += 1
    pieces = psum_ref.shape[0]
    rows = patch // pieces

    def hand_out_probe(s, carry):
        piece = piece_of(s, device)
        psum_ref[s] = pacc[:, pl.ds(pl.multiple_of(piece * rows, rows), rows), :].astype(BF16)
        return carry

    lax.fori_loop(0, pieces, hand_out_probe, 0)

def move(value, steps):
    count = lax.axis_size("tile")
    pairs = []
    for i in range(count):
        kind, step = steps[i % 2]
        if kind == "bit":
            to = i ^ step
        else:
            to = i + (step if (i // 2) % 2 == 0 else -step)
        if 0 <= to < count:
            pairs.append((i, to))
    return lax.ppermute(value, "tile", pairs)


def swap_bits(value, bit0, bit1):
    return move(value, (("bit", bit0), ("bit", bit1)))


def to_sibling(value):
    return swap_bits(value, 1, 1)


def piece_of(s, device):
    core = device & 1
    other = s >> (BITS - 1)
    mine = core ^ other
    away0 = sum(((s >> (BITS - 2 - j)) & 1) * bit for j, bit in enumerate(PROBE_BITS[0]))
    away1 = sum(((s >> (BITS - 2 - j)) & 1) * bit for j, bit in enumerate(PROBE_BITS[1]))
    return ((device & (2**BITS - 1)) ^ other) ^ jnp.where(mine == 0, away0, away1)


def place(row, col, first_row, tile_rows, window_tiles, patch, width):
    block_tiles = (patch + tile_rows - 1) // tile_rows + 1
    local_row = row - first_row
    tile = jnp.clip(local_row // tile_rows, 0, window_tiles - block_tiles)
    block = jnp.minimum(col // LANES, (width - patch - LANES) // LANES)
    return tile, local_row - tile * tile_rows, block, col - block * LANES


def pack_kernel(pos_ref, obj_ref, out_ref):
    tile_rows, width = obj_ref.shape[1:]
    both = 2 * tile_rows
    for q in range(width // LANES):
        part = obj_ref[:, :, q * LANES : (q + 1) * LANES].reshape(both, LANES)
        out_ref[q * both : (q + 1) * both] = part.astype(BF16)
    lane = lax.broadcasted_iota(jnp.int32, (HEAD_ROWS, LANES), 1)
    head = jnp.zeros((HEAD_ROWS, LANES), jnp.int32)
    for k in range(pos_ref.shape[0]):
        value = pos_ref[k]
        head = jnp.where(lane == 2 * k, value // BASE, head)
        head = jnp.where(lane == 2 * k + 1, lax.rem(value, BASE), head)
    out_ref[width // LANES * both :] = head.astype(F32).astype(BF16)


def coverage_kernel(tile_rows, per_holder, index_ref, heads_ref, probe_ref, out_ref, padded, digits, pos_ref):
    modes, patch = probe_ref.shape[1], probe_ref.shape[2]
    width = out_ref.shape[1]
    slots = heads_ref.shape[0]
    me, count = index_ref[slots], index_ref[slots + 1]
    heads = heads_ref[...].astype(F32)
    for s in range(slots):
        row = heads[s, :SUBLANES]
        digits[s] = (row * BASE + pltpu.roll(row, LANES - 1, 1)).astype(jnp.int32)
    pltpu.sync_copy(digits, pos_ref)
    total = jnp.zeros((patch, patch), F32)
    for m in range(modes):
        total = total + (probe_ref[0, m] * probe_ref[0, m] + probe_ref[1, m] * probe_ref[1, m])
    padded[...] = jnp.zeros(padded.shape, F32)
    for q in range(patch // LANES):
        padded[q, tile_rows : tile_rows + patch] = total[:, q * LANES : (q + 1) * LANES]
    sublane = lax.broadcasted_iota(jnp.int32, (tile_rows // SUBLANES, SUBLANES, LANES), 1)
    lanes = lax.broadcasted_iota(jnp.int32, (tile_rows, LANES), 1)
    out_ref[...] = jnp.ones(out_ref.shape, F32)

    def visit(k, carry):
        s, p = k // per_holder, lax.rem(k, per_holder)
        holder = index_ref[s]
        row, col = pos_ref[s, 0, 4 * p], pos_ref[s, 0, 4 * p + 2]
        at = me * tile_rows - row + tile_rows
        col_block = jnp.minimum(col // LANES, (width - patch - LANES) // LANES)
        there = jnp.logical_and(holder >= 0, holder < count)

        @pl.when(jnp.logical_and(there, jnp.logical_and(at > 0, at < tile_rows + patch)))
        def _():
            sub = lax.rem(at, SUBLANES)
            lane = col - col_block * LANES
            turned = []
            for q in range(patch // LANES):
                rows = padded[q, pl.ds(pl.multiple_of(at - sub, SUBLANES), tile_rows + SUBLANES), :]
                rows = pltpu.roll(rows.reshape(-1, SUBLANES, LANES), lax.rem(SUBLANES - sub, SUBLANES), 1)
                rows = jnp.where(sublane < SUBLANES - sub, rows[:-1], rows[1:]).reshape(tile_rows, LANES)
                turned.append(pltpu.roll(rows, lax.rem(lane, LANES), 1))
            for q in range(patch // LANES + 1):
                here = turned[q] if q < patch // LANES else jnp.zeros((tile_rows, LANES), F32)
                before = turned[q - 1] if q > 0 else jnp.zeros((tile_rows, LANES), F32)
                cols = pl.ds(pl.multiple_of((col_block + q) * LANES, LANES), LANES)
                out_ref[:, cols] = out_ref[:, cols] + jnp.where(lanes >= lane, here, before)

        return carry

    lax.fori_loop(0, slots * per_holder, visit, 0)


def order_kernel(order_ref, meas_ref, out_ref):
    turn = order_ref[...]
    for p in range(meas_ref.shape[0]):
        rows = jnp.dot(turn, meas_ref[p], preferred_element_type=F32, precision=lax.Precision.HIGHEST)
        out_ref[p] = lax.dot_general(
            rows, turn, (((1,), (1,)), ((), ())), preferred_element_type=F32, precision=lax.Precision.HIGHEST
        )


def unpack_kernel(index_ref, pieces_ref, out_ref):
    pieces, planes, rows, cols = pieces_ref.shape
    modes = out_ref.shape[1]
    device = index_ref[0]

    def visit(s, carry):
        piece = piece_of(s, device)
        at = pl.ds(pl.multiple_of(piece * rows, rows), rows)
        value = pieces_ref[s].astype(F32)
        for c in range(2):
            out_ref[c, :, at, :] = value[c * modes : (c + 1) * modes]
        return carry

    lax.fori_loop(0, pieces, visit, 0)


VMEM = pl.BlockSpec(memory_space=pltpu.VMEM)
SMEM = pl.BlockSpec(memory_space=pltpu.SMEM)


def call(kernel, name, out_shape, in_specs, limit, flops, bytes_accessed, scratch=()):
    return pl.pallas_call(
        kernel,
        out_shape=out_shape,
        in_specs=in_specs,
        out_specs=jax.tree.map(lambda _: VMEM, out_shape),
        scratch_shapes=list(scratch),
        compiler_params=pltpu.CompilerParams(vmem_limit_bytes=limit * MIB),
        cost_estimate=pl.CostEstimate(flops=flops, bytes_accessed=bytes_accessed, transcendentals=0),
        name=name,
    )


def add(a, b):
    return (a.astype(F32) + b.astype(F32)).astype(BF16)


def local(object_field, probe_modes, positions, intensity):
    tile_rows, width = object_field.shape[1:]
    modes, patch = probe_modes.shape[1:3]
    per_holder = positions.shape[0]
    count = lax.axis_size("tile")
    me = lax.axis_index("tile")
    core, chip = me % 2, me // 2
    block_rows = ((patch + tile_rows - 1) // tile_rows + 1) * tile_rows
    both = 2 * tile_rows
    tiles = 2 + 4 * REACH_CHIPS
    first_core = core == 0
    mine_first = positions.reshape(-1)

    own = call(
        pack_kernel, "pack", jax.ShapeDtypeStruct((width // LANES * both + HEAD_ROWS, LANES), BF16), [SMEM, VMEM],
        8, 1_000_000, 1_000_000,
    )(mine_first, object_field)
    pair = jnp.concatenate([own, to_sibling(own)])
    first = move(pair, (("shift", -4), ("bit", 2)))
    second = move(jnp.where(first_core, first, pair), (("bit", 2), ("shift", 4)))
    third = move(jnp.where(first_core, second, first), (("shift", 4), ("shift", -4)))
    brought = [first, second, third]
    window = jnp.concatenate([pair] + brought + [to_sibling(v) for v in brought]).reshape(tiles, -1, LANES)

    cases = []
    for c in range(2):
        slots = [(0, c), (0, 1 - c)]
        slots += [(away, t) for away in BROUGHT[c] for t in (c, 1 - c)]
        slots += [(away, t) for away in BROUGHT[1 - c] for t in (1 - c, c)]
        order = [(w // 2 - REACH_CHIPS, w % 2) for w in range(tiles)]
        cases.append(
            [
                np.array([away for away, _ in slots]),
                np.array([t for _, t in slots]),
                np.array([slots.index((away, t)) for away, t in order]),
                np.array([slots.index((-away, t)) for away, t in order]),
            ]
        )
    aways, cores, even_where, odd_where = [jnp.where(first_core, u, v) for u, v in zip(*cases, strict=True)]
    even = chip % 2 == 0
    holders = 2 * (chip + jnp.where(even, aways, -aways)) + cores
    index = jnp.concatenate([holders, me[None], jnp.full((1,), count)]).astype(jnp.int32)
    first_row = (2 * (chip - REACH_CHIPS)) * tile_rows
    where = jnp.concatenate([jnp.where(even, even_where, odd_where), first_row[None], me[None]]).astype(jnp.int32)

    coverage = call(
        lambda *refs: coverage_kernel(tile_rows, per_holder, *refs), "coverage",
        jax.ShapeDtypeStruct((tile_rows, width), F32), [SMEM, VMEM, VMEM],
        8, 10_000_000, 3_000_000,
        [
            pltpu.VMEM((patch // LANES, patch + 2 * tile_rows + 16, LANES), F32),
            pltpu.VMEM((tiles, SUBLANES, LANES), jnp.int32),
            pltpu.SMEM((tiles, SUBLANES, LANES), jnp.int32),
        ],
    )(index, window[:, -HEAD_ROWS:], probe_modes)

    right, left = real_tables(patch)
    ordered = call(
        order_kernel, "order", jax.ShapeDtypeStruct(intensity.shape, F32), [VMEM, VMEM], 8, 2_000_000_000, 2_000_000
    )(jnp.asarray(frequency_order(patch)), intensity)

    pieces = 2**BITS
    rows = patch // pieces
    planes = 2 * modes + 1
    cols = patch // LANES
    one, two = [jax.ShapeDtypeStruct((n * both, width), BF16) for n in (1, 2)]
    own_sum, sibling_sum, *sums, psum = call(
        lambda *refs: positions_kernel(tile_rows, *refs), "positions",
        (one,) * 2 + (two,) * 6 + (jax.ShapeDtypeStruct((pieces, planes, rows, patch), BF16),),
        [SMEM, SMEM, VMEM, VMEM, VMEM, VMEM, VMEM],
        24, 10_000_000_000, 20_000_000,
        [
            pltpu.VMEM((2, cols + 1, block_rows + 16, LANES), F32),
            pltpu.VMEM((2, patch, patch), F32),
            pltpu.VMEM((2, modes, patch, patch), F32),
            pltpu.VMEM((tiles, both, width), BF16),
            pltpu.VMEM((2, cols + 1, block_rows + 16, LANES), F32),
            pltpu.VMEM((planes, patch, patch), F32),
        ],
    )(mine_first, where, window, probe_modes, ordered, right, left)

    sum1, sum2, sum3 = [add(sums[j], to_sibling(sums[REACH_CHIPS + j])) for j in range(REACH_CHIPS)]
    came3 = move(sum3, (("shift", -4), ("shift", 4)))
    sum2 = add(sum2, jnp.where(first_core, came3, 0))
    came2 = move(sum2, (("bit", 2), ("shift", -4)))
    sum1 = add(sum1, jnp.where(first_core, came2, came3))
    came1 = move(sum1, (("shift", 4), ("bit", 2)))
    came = came1.astype(F32) + jnp.where(first_core, 0, came2).astype(F32)
    total = own_sum.astype(F32) + came[:both]
    total = total + to_sibling((sibling_sum.astype(F32) + came[both:]).astype(BF16)).astype(F32)
    object_step = total.reshape(2, tile_rows, width) / coverage[None]

    psum = psum.reshape((2,) * BITS + (planes, rows, patch))
    psum = add(psum[0], to_sibling(psum[1]))
    (a0, b0, c0), (a1, b1, c1) = PROBE_BITS
    psum = add(psum[0], swap_bits(psum[1], a0, a1))
    psum = add(psum[0], swap_bits(psum[1], b0, b1))
    psum = add(psum, swap_bits(psum, c0, c1)[::-1])
    bit = 1 << BITS
    while bit < count:
        psum = add(psum, swap_bits(psum, bit, bit))
        bit *= 2
    psum = psum.astype(F32)
    pstep = (psum[:, : 2 * modes] / jnp.sqrt(1.0 + psum[:, 2 * modes :])).astype(BF16)
    pstep = jnp.stack([pstep, swap_bits(pstep, b0, b1)])
    pstep = jnp.stack([pstep, swap_bits(pstep, a0, a1)])
    pstep = jnp.stack([pstep, to_sibling(pstep)])
    probe_step = call(
        unpack_kernel, "probe_unpack", jax.ShapeDtypeStruct(probe_modes.shape, F32), [SMEM, VMEM], 8, 1_000_000, 3_000_000
    )(me[None].astype(jnp.int32), pstep.reshape(pieces, 2 * modes, rows, patch))
    return (object_step, probe_step)


def solution(mesh):
    in_specs = (
        P(None, ("grp", "tile"), None),
        P(None, "grp", None, None),
        P(("grp", "tile"), None),
        P(("grp", "tile"), None, None),
    )
    out_specs = (P(None, ("grp", "tile"), None), P(None, "grp", None, None))
    return jax.shard_map(local, mesh=mesh, in_specs=in_specs, out_specs=out_specs, check_vma=False)
```

```python
import math

import jax
import jax.numpy as jnp
import numpy as np
from jax import lax
from jax.experimental import pallas as pl
from jax.experimental.pallas import tpu as pltpu
from jax.sharding import PartitionSpec as P

F32 = jnp.float32
BF16 = jnp.bfloat16
LANES = 128
SUBLANES = 8
MIB = 1024 * 1024
BROUGHT = ((2, -1, -3), (1, -2, 3))
REACH_CHIPS = 3
PROBE_BITS = ((2, 4, 8), (4, 8, 2))
BITS = 4
HEAD_ROWS = 16
BASE = 128


def real_tables(size):
    steps = np.arange(size)
    phase = (steps[:, None] * steps[None, :] % size) * (2.0 * math.pi / size)
    factor = 1.0 / math.sqrt(size)
    cos_table, sine_table = np.cos(phase) * factor, np.sin(phase) * factor
    mid = size // 2
    table = np.concatenate([cos_table[:, :mid], cos_table[:, mid : mid + 1], sine_table[:, 1:mid]], axis=1)
    return jnp.asarray(table, BF16), jnp.asarray(table.T.copy(), BF16)


def frequency_order(size):
    mid = size // 2
    order = np.concatenate([np.arange(mid), [mid], np.arange(size - 1, mid, -1)])
    return np.eye(size, dtype=np.float32)[order]


def dot(a, b):
    return jnp.dot(a, b, preferred_element_type=F32)


def with_first_row(first, rest):
    row = lax.broadcasted_iota(jnp.int32, (SUBLANES, rest.shape[1]), 0)
    top = jnp.where(row == 0, first[:SUBLANES], rest[:SUBLANES])
    return jnp.concatenate([top, rest[SUBLANES:]], axis=0)


def with_first_lane(first, rest):
    lane = lax.broadcasted_iota(jnp.int32, rest.shape, 1)
    return jnp.where(lane == 0, first, rest)


def unfold(pick, axis, u, v):
    mid = u.shape[axis] // 2
    part = (lambda x, i: x[i * mid : (i + 1) * mid]) if axis == 0 else (lambda x, i: x[:, i * mid : (i + 1) * mid])
    u1, u2, v1, v2 = part(u, 0), part(u, 1), part(v, 0), part(v, 1)
    real = jnp.concatenate([pick(u1, u1 + v2), pick(u2, u1 - v2)], axis=axis)
    imag = jnp.concatenate([pick(v1, v1 - u2), pick(v2, v1 + u2)], axis=axis)
    return real, imag


def fold(pick, axis, real, imag):
    mid = real.shape[axis] // 2
    part = (lambda x, i: x[i * mid : (i + 1) * mid]) if axis == 0 else (lambda x, i: x[:, i * mid : (i + 1) * mid])
    r1, r2, i1, i2 = part(real, 0), part(real, 1), part(imag, 0), part(imag, 1)
    a = jnp.concatenate([pick(r1, r1 + r2), pick(r2, i2 - i1)], axis=axis)
    b = jnp.concatenate([pick(i1, i1 + i2), pick(i2, r1 - r2)], axis=axis)
    return a.astype(BF16), b.astype(BF16)


def positions_kernel(
    tile_rows, pos_ref, where_ref, probe_ref, meas_ref, right_ref, left_ref, *rest
):
    *tile_refs, psum_ref, win_ref, raw, obj, far, sums, grad, pacc = rest
    slots = len(tile_refs) // 2
    in_refs, out_refs = tile_refs[:slots], tile_refs[slots:]
    per_holder = meas_ref.shape[0]
    modes = probe_ref.shape[1]
    patch = probe_ref.shape[2]
    both = 2 * tile_rows
    width = sums.shape[2]
    block_tiles = (patch + tile_rows - 1) // tile_rows + 1
    block_rows = block_tiles * tile_rows
    first_row = where_ref[slots]
    device = where_ref[slots + 1]
    tall = patch // SUBLANES
    sublane = lax.broadcasted_iota(jnp.int32, (tall + 1, SUBLANES, LANES), 1)
    lanes = lax.broadcasted_iota(jnp.int32, (patch, LANES), 1)
    cols = patch // LANES

    for t in range(slots):
        win_ref[t] = in_refs[t][: win_ref.shape[1]]
        sums[t] = jnp.zeros(sums.shape[1:], BF16)
    pacc[...] = jnp.zeros(pacc.shape, F32)

    def visit(p, carry):
        tile, off, block, lane = place(
            pos_ref[0, p], pos_ref[1, p], first_row, tile_rows, slots, patch, width
        )
        sub = lax.rem(off, SUBLANES)
        base = pl.multiple_of(off - sub, SUBLANES)
        for j in range(block_tiles):
            for q in range(cols + 1):
                at = pl.ds(pl.multiple_of((block + q) * both, 16), both)
                part = win_ref[where_ref[tile + j], at, :].astype(F32)
                raw[0, q, j * tile_rows : (j + 1) * tile_rows] = part[:tile_rows]
                raw[1, q, j * tile_rows : (j + 1) * tile_rows] = part[tile_rows:]
        for c in range(2):
            turned = []
            for q in range(cols + 1):
                rows = raw[c, q, pl.ds(base, patch + SUBLANES), :].reshape(tall + 1, SUBLANES, LANES)
                rows = pltpu.roll(rows, lax.rem(SUBLANES - sub, SUBLANES), 1)
                rows = jnp.where(sublane[:tall] < SUBLANES - sub, rows[:tall], rows[1:])
                turned.append(pltpu.roll(rows.reshape(patch, LANES), lax.rem(LANES - lane, LANES), 1))
            for q in range(cols):
                obj[c, :, q * LANES : (q + 1) * LANES] = jnp.where(lanes < LANES - lane, turned[q], turned[q + 1])
        pacc[2 * modes] = pacc[2 * modes] + (obj[0] * obj[0] + obj[1] * obj[1])
        model = jnp.ones((patch, patch), F32)
        for m in range(modes):
            probe_real, probe_imag = probe_ref[0, m], probe_ref[1, m]
            exit_real = (probe_real * obj[0] - probe_imag * obj[1]).astype(BF16)
            exit_imag = (probe_real * obj[1] + probe_imag * obj[0]).astype(BF16)
            half_real, half_imag = unfold(
                with_first_lane, 1, dot(exit_real, right_ref[...]), dot(exit_imag, right_ref[...])
            )
            far_real, far_imag = unfold(
                with_first_row, 0, dot(left_ref[...], half_real.astype(BF16)), dot(left_ref[...], half_imag.astype(BF16))
            )
            far[0, m] = far_real
            far[1, m] = far_imag
            model = model + (far_real * far_real + far_imag * far_imag)
        factor = jnp.sqrt(meas_ref[p] / model) - 1.0
        grad_real = jnp.zeros((patch, patch), F32)
        grad_imag = jnp.zeros((patch, patch), F32)
        for m in range(modes):
            a, b = fold(with_first_lane, 1, far[0, m] * factor, far[1, m] * factor)
            a, b = fold(with_first_row, 0, dot(a, left_ref[...]), dot(b, left_ref[...]))
            change_real, change_imag = dot(right_ref[...], a), dot(right_ref[...], b)
            probe_real, probe_imag = probe_ref[0, m], probe_ref[1, m]
            grad_real = grad_real + (probe_real * change_real + probe_imag * change_imag)
            grad_imag = grad_imag + (probe_real * change_imag - probe_imag * change_real)
            pacc[m] = pacc[m] + (obj[0] * change_real + obj[1] * change_imag)
            pacc[modes + m] = pacc[modes + m] + (obj[0] * change_imag - obj[1] * change_real)
        edge = jnp.zeros((1, SUBLANES, LANES), F32)
        for c, value in enumerate((grad_real, grad_imag)):
            turned = [
                pltpu.roll(value[:, q * LANES : (q + 1) * LANES], lax.rem(lane, LANES), 1) for q in range(cols)
            ]
            for q in range(cols + 1):
                here = turned[q] if q < cols else jnp.zeros((patch, LANES), F32)
                before = turned[q - 1] if q > 0 else jnp.zeros((patch, LANES), F32)
                wide = jnp.where(lanes >= lane, here, before).reshape(tall, SUBLANES, LANES)
                wide = pltpu.roll(wide, sub, 1)
                wide = jnp.where(
                    sublane >= sub, jnp.concatenate([wide, edge], axis=0), jnp.concatenate([edge, wide], axis=0)
                )
                grad[c, q] = jnp.zeros(grad.shape[2:], F32)
                grad[c, q, pl.ds(base, patch + SUBLANES), :] = wide.reshape(patch + SUBLANES, LANES)
        for j in range(block_tiles):
            slot = where_ref[tile + j]
            rows = slice(j * tile_rows, (j + 1) * tile_rows)
            for q in range(cols + 1):
                at = pl.ds(pl.multiple_of((block + q) * LANES, LANES), LANES)
                part = jnp.concatenate([grad[0, q, rows], grad[1, q, rows]], axis=0)
                sums[slot, :, at] = (sums[slot, :, at].astype(F32) + part).astype(BF16)
        return carry

    lax.fori_loop(0, per_holder, visit, 0)

    for t in range(slots):
        out_refs[t][...] = sums[t]
    pieces = psum_ref.shape[0]
    rows = patch // pieces

    def hand_out_probe(s, carry):
        piece = piece_of(s, device)
        psum_ref[s] = pacc[:, pl.ds(pl.multiple_of(piece * rows, rows), rows), :].astype(BF16)
        return carry

    lax.fori_loop(0, pieces, hand_out_probe, 0)

def move(value, steps):
    count = lax.axis_size("tile")
    pairs = []
    for i in range(count):
        kind, step = steps[i % 2]
        if kind == "bit":
            to = i ^ step
        else:
            to = i + (step if (i // 2) % 2 == 0 else -step)
        if 0 <= to < count:
            pairs.append((i, to))
    return lax.ppermute(value, "tile", pairs)


def swap_bits(value, bit0, bit1):
    return move(value, (("bit", bit0), ("bit", bit1)))


def to_sibling(value):
    return swap_bits(value, 1, 1)


def piece_of(s, device):
    core = device & 1
    other = s >> (BITS - 1)
    mine = core ^ other
    away0 = sum(((s >> (BITS - 2 - j)) & 1) * bit for j, bit in enumerate(PROBE_BITS[0]))
    away1 = sum(((s >> (BITS - 2 - j)) & 1) * bit for j, bit in enumerate(PROBE_BITS[1]))
    return ((device & (2**BITS - 1)) ^ other) ^ jnp.where(mine == 0, away0, away1)


def place(row, col, first_row, tile_rows, window_tiles, patch, width):
    block_tiles = (patch + tile_rows - 1) // tile_rows + 1
    local_row = row - first_row
    tile = jnp.clip(local_row // tile_rows, 0, window_tiles - block_tiles)
    block = jnp.minimum(col // LANES, (width - patch - LANES) // LANES)
    return tile, local_row - tile * tile_rows, block, col - block * LANES


def pack_kernel(pos_ref, obj_ref, out_ref):
    tile_rows, width = obj_ref.shape[1:]
    both = 2 * tile_rows
    for q in range(width // LANES):
        part = obj_ref[:, :, q * LANES : (q + 1) * LANES].reshape(both, LANES)
        out_ref[q * both : (q + 1) * both] = part.astype(BF16)
    lane = lax.broadcasted_iota(jnp.int32, (HEAD_ROWS, LANES), 1)
    head = jnp.zeros((HEAD_ROWS, LANES), jnp.int32)
    for k in range(2 * pos_ref.shape[1]):
        value = pos_ref[k % 2, k // 2]
        head = jnp.where(lane == 2 * k, value // BASE, head)
        head = jnp.where(lane == 2 * k + 1, lax.rem(value, BASE), head)
    out_ref[width // LANES * both :] = head.astype(F32).astype(BF16)


def coverage_kernel(tile_rows, per_holder, index_ref, heads_ref, probe_ref, out_ref, padded, digits, pos_ref):
    modes, patch = probe_ref.shape[1], probe_ref.shape[2]
    width = out_ref.shape[1]
    slots = heads_ref.shape[0]
    me, count = index_ref[slots], index_ref[slots + 1]
    heads = heads_ref[...].astype(F32)
    for s in range(slots):
        row = heads[s, :SUBLANES]
        digits[s] = (row * BASE + pltpu.roll(row, LANES - 1, 1)).astype(jnp.int32)
    pltpu.sync_copy(digits, pos_ref)
    total = jnp.zeros((patch, patch), F32)
    for m in range(modes):
        total = total + (probe_ref[0, m] * probe_ref[0, m] + probe_ref[1, m] * probe_ref[1, m])
    padded[...] = jnp.zeros(padded.shape, F32)
    for q in range(patch // LANES):
        padded[q, tile_rows : tile_rows + patch] = total[:, q * LANES : (q + 1) * LANES]
    sublane = lax.broadcasted_iota(jnp.int32, (tile_rows // SUBLANES, SUBLANES, LANES), 1)
    lanes = lax.broadcasted_iota(jnp.int32, (tile_rows, LANES), 1)
    out_ref[...] = jnp.ones(out_ref.shape, F32)

    def visit(k, carry):
        s, p = k // per_holder, lax.rem(k, per_holder)
        holder = index_ref[s]
        row, col = pos_ref[s, 0, 4 * p], pos_ref[s, 0, 4 * p + 2]
        at = me * tile_rows - row + tile_rows
        col_block = jnp.minimum(col // LANES, (width - patch - LANES) // LANES)
        there = jnp.logical_and(holder >= 0, holder < count)

        @pl.when(jnp.logical_and(there, jnp.logical_and(at > 0, at < tile_rows + patch)))
        def _():
            sub = lax.rem(at, SUBLANES)
            lane = col - col_block * LANES
            turned = []
            for q in range(patch // LANES):
                rows = padded[q, pl.ds(pl.multiple_of(at - sub, SUBLANES), tile_rows + SUBLANES), :]
                rows = pltpu.roll(rows.reshape(-1, SUBLANES, LANES), lax.rem(SUBLANES - sub, SUBLANES), 1)
                rows = jnp.where(sublane < SUBLANES - sub, rows[:-1], rows[1:]).reshape(tile_rows, LANES)
                turned.append(pltpu.roll(rows, lax.rem(lane, LANES), 1))
            for q in range(patch // LANES + 1):
                here = turned[q] if q < patch // LANES else jnp.zeros((tile_rows, LANES), F32)
                before = turned[q - 1] if q > 0 else jnp.zeros((tile_rows, LANES), F32)
                cols = pl.ds(pl.multiple_of((col_block + q) * LANES, LANES), LANES)
                out_ref[:, cols] = out_ref[:, cols] + jnp.where(lanes >= lane, here, before)

        return carry

    lax.fori_loop(0, slots * per_holder, visit, 0)


def order_kernel(order_ref, meas_ref, out_ref):
    turn = order_ref[...]
    for p in range(meas_ref.shape[0]):
        rows = jnp.dot(turn, meas_ref[p], preferred_element_type=F32, precision=lax.Precision.HIGHEST)
        out_ref[p] = lax.dot_general(
            rows, turn, (((1,), (1,)), ((), ())), preferred_element_type=F32, precision=lax.Precision.HIGHEST
        )


def unpack_kernel(index_ref, pieces_ref, out_ref):
    pieces, planes, rows, cols = pieces_ref.shape
    modes = out_ref.shape[1]
    device = index_ref[0]

    def visit(s, carry):
        piece = piece_of(s, device)
        at = pl.ds(pl.multiple_of(piece * rows, rows), rows)
        value = pieces_ref[s].astype(F32)
        for c in range(2):
            out_ref[c, :, at, :] = value[c * modes : (c + 1) * modes]
        return carry

    lax.fori_loop(0, pieces, visit, 0)


VMEM = pl.BlockSpec(memory_space=pltpu.VMEM)
SMEM = pl.BlockSpec(memory_space=pltpu.SMEM)


def call(kernel, name, out_shape, in_specs, limit, flops, bytes_accessed, scratch=()):
    return pl.pallas_call(
        kernel,
        out_shape=out_shape,
        in_specs=in_specs,
        out_specs=jax.tree.map(lambda _: VMEM, out_shape),
        scratch_shapes=list(scratch),
        compiler_params=pltpu.CompilerParams(vmem_limit_bytes=limit * MIB),
        cost_estimate=pl.CostEstimate(flops=flops, bytes_accessed=bytes_accessed, transcendentals=0),
        name=name,
    )


def add(a, b):
    return (a.astype(F32) + b.astype(F32)).astype(BF16)


def local(object_field, probe_modes, positions, intensity):
    tile_rows, width = object_field.shape[1:]
    modes, patch = probe_modes.shape[1:3]
    per_holder = positions.shape[0]
    count = lax.axis_size("tile")
    me = lax.axis_index("tile")
    core, chip = me % 2, me // 2
    block_rows = ((patch + tile_rows - 1) // tile_rows + 1) * tile_rows
    both = 2 * tile_rows
    tiles = 2 + 4 * REACH_CHIPS
    first_core = core == 0
    mine_first = positions.T

    own = call(
        pack_kernel, "pack", jax.ShapeDtypeStruct((width // LANES * both + HEAD_ROWS, LANES), BF16), [SMEM, VMEM],
        8, 1_000_000, 1_000_000,
    )(mine_first, object_field)
    pair = [own, to_sibling(own)]
    first = [move(v, (("shift", -4), ("bit", 2))) for v in pair]
    second = [move(jnp.where(first_core, u, v), (("bit", 2), ("shift", 4))) for u, v in zip(first, pair)]
    third = [move(jnp.where(first_core, u, v), (("shift", 4), ("shift", -4))) for u, v in zip(second, first)]
    brought = first + second + third
    window = pair + brought + [to_sibling(v) for v in brought]

    cases = []
    for c in range(2):
        slots = [(0, c), (0, 1 - c)]
        slots += [(away, t) for away in BROUGHT[c] for t in (c, 1 - c)]
        slots += [(away, t) for away in BROUGHT[1 - c] for t in (1 - c, c)]
        order = [(w // 2 - REACH_CHIPS, w % 2) for w in range(tiles)]
        cases.append(
            [
                np.array([away for away, _ in slots]),
                np.array([t for _, t in slots]),
                np.array([slots.index((away, t)) for away, t in order]),
                np.array([slots.index((-away, t)) for away, t in order]),
            ]
        )
    aways, cores, even_where, odd_where = [jnp.where(first_core, u, v) for u, v in zip(*cases, strict=True)]
    even = chip % 2 == 0
    holders = 2 * (chip + jnp.where(even, aways, -aways)) + cores
    index = jnp.concatenate([holders, me[None], jnp.full((1,), count)]).astype(jnp.int32)
    first_row = (2 * (chip - REACH_CHIPS)) * tile_rows
    where = jnp.concatenate([jnp.where(even, even_where, odd_where), first_row[None], me[None]]).astype(jnp.int32)

    right, left = real_tables(patch)
    ordered = call(
        order_kernel, "order", jax.ShapeDtypeStruct(intensity.shape, F32), [VMEM, VMEM], 8, 2_000_000_000, 2_000_000
    )(jnp.asarray(frequency_order(patch)), intensity)

    pieces = 2**BITS
    rows = patch // pieces
    planes = 2 * modes + 1
    cols = patch // LANES
    *sums, psum = call(
        lambda *refs: positions_kernel(tile_rows, *refs), "positions",
        (jax.ShapeDtypeStruct((both, width), BF16),) * tiles + (jax.ShapeDtypeStruct((pieces, planes, rows, patch), BF16),),
        [SMEM, SMEM] + [VMEM] * (4 + tiles),
        24, 10_000_000_000, 20_000_000,
        [
            pltpu.VMEM((tiles, width // LANES * both, LANES), BF16),
            pltpu.VMEM((2, cols + 1, block_rows + 16, LANES), F32),
            pltpu.VMEM((2, patch, patch), F32),
            pltpu.VMEM((2, modes, patch, patch), F32),
            pltpu.VMEM((tiles, both, width), BF16),
            pltpu.VMEM((2, cols + 1, block_rows + 16, LANES), F32),
            pltpu.VMEM((planes, patch, patch), F32),
        ],
    )(mine_first, where, probe_modes, ordered, right, left, *window)

    own_sum, sibling_sum, *sums = sums
    kept, given = sums[: 2 * REACH_CHIPS], sums[2 * REACH_CHIPS :]
    sums = [None] * 2 * REACH_CHIPS
    for j in (5, 4, 3, 2, 1, 0):
        sums[j] = add(kept[j], to_sibling(given[j]))
    came3 = [move(sums[4 + j], (("shift", -4), ("shift", 4))) for j in (1, 0)]
    sum2 = [add(sums[2 + j], jnp.where(first_core, v, 0)) for j, v in zip((1, 0), came3)]
    came2 = [move(v, (("bit", 2), ("shift", -4))) for v in sum2]
    sum1 = [add(sums[j], jnp.where(first_core, u, v)) for j, u, v in zip((1, 0), came2, came3)]
    came1 = [move(v, (("shift", 4), ("bit", 2))) for v in sum1]
    came = [u.astype(F32) + jnp.where(first_core, 0, v).astype(F32) for u, v in zip(came1, came2)]
    total = own_sum.astype(F32) + to_sibling((sibling_sum.astype(F32) + came[0]).astype(BF16)).astype(F32) + came[1]
    heads, _ = lax.optimization_barrier((jnp.stack([v[-HEAD_ROWS:] for v in window]), sums[5]))
    coverage = call(
        lambda *refs: coverage_kernel(tile_rows, per_holder, *refs), "coverage",
        jax.ShapeDtypeStruct((tile_rows, width), F32), [SMEM, VMEM, VMEM],
        8, 10_000_000, 3_000_000,
        [
            pltpu.VMEM((patch // LANES, patch + 2 * tile_rows + 16, LANES), F32),
            pltpu.VMEM((tiles, SUBLANES, LANES), jnp.int32),
            pltpu.SMEM((tiles, SUBLANES, LANES), jnp.int32),
        ],
    )(index, heads, probe_modes)

    object_step = total.reshape(2, tile_rows, width) / coverage[None]

    psum = psum.reshape((2,) * BITS + (planes, rows, patch))
    psum = add(psum[0], to_sibling(psum[1]))
    (a0, b0, c0), (a1, b1, c1) = PROBE_BITS
    psum = add(psum[0], swap_bits(psum[1], a0, a1))
    psum = add(psum[0], swap_bits(psum[1], b0, b1))
    psum = add(psum, swap_bits(psum, c0, c1)[::-1])
    bit = 1 << BITS
    while bit < count:
        psum = add(psum, swap_bits(psum, bit, bit))
        bit *= 2
    psum = psum.astype(F32)
    pstep = (psum[:, : 2 * modes] / jnp.sqrt(1.0 + psum[:, 2 * modes :])).astype(BF16)
    pstep = jnp.stack([pstep, swap_bits(pstep, b0, b1)])
    pstep = jnp.stack([pstep, swap_bits(pstep, a0, a1)])
    pstep = jnp.stack([pstep, to_sibling(pstep)])
    probe_step = call(
        unpack_kernel, "probe_unpack", jax.ShapeDtypeStruct(probe_modes.shape, F32), [SMEM, VMEM], 8, 1_000_000, 3_000_000
    )(me[None].astype(jnp.int32), pstep.reshape(pieces, 2 * modes, rows, patch))
    return (object_step, probe_step)


def solution(mesh):
    in_specs = (
        P(None, ("grp", "tile"), None),
        P(None, "grp", None, None),
        P(("grp", "tile"), None),
        P(("grp", "tile"), None, None),
    )
    out_specs = (P(None, ("grp", "tile"), None), P(None, "grp", None, None))
    return jax.shard_map(local, mesh=mesh, in_specs=in_specs, out_specs=out_specs, check_vma=False)
```

```python
import math

import jax
import jax.numpy as jnp
import numpy as np
from jax import lax
from jax.experimental import pallas as pl
from jax.experimental.pallas import tpu as pltpu
from jax.sharding import PartitionSpec as P

F32 = jnp.float32
BF16 = jnp.bfloat16
LANES = 128
SUBLANES = 8
MIB = 1024 * 1024
BROUGHT = ((2, -1, -3), (1, -2, 3))
REACH_CHIPS = 3
PROBE_BITS = ((2, 4, 8), (4, 8, 2))
BITS = 4
HEAD_ROWS = 16
BASE = 128


def real_tables(size):
    steps = np.arange(size)
    phase = (steps[:, None] * steps[None, :] % size) * (2.0 * math.pi / size)
    factor = 1.0 / math.sqrt(size)
    cos_table, sine_table = np.cos(phase) * factor, np.sin(phase) * factor
    mid = size // 2
    table = np.concatenate([cos_table[:, :mid], cos_table[:, mid : mid + 1], sine_table[:, 1:mid]], axis=1)
    return jnp.asarray(table, BF16), jnp.asarray(table.T.copy(), BF16)


def frequency_order(size):
    mid = size // 2
    order = np.concatenate([np.arange(mid), [mid], np.arange(size - 1, mid, -1)])
    return np.eye(size, dtype=np.float32)[order]


def dot(a, b):
    return jnp.dot(a, b, preferred_element_type=F32)


def with_first_row(first, rest):
    row = lax.broadcasted_iota(jnp.int32, (SUBLANES, rest.shape[1]), 0)
    top = jnp.where(row == 0, first[:SUBLANES], rest[:SUBLANES])
    return jnp.concatenate([top, rest[SUBLANES:]], axis=0)


def with_first_lane(first, rest):
    lane = lax.broadcasted_iota(jnp.int32, rest.shape, 1)
    return jnp.where(lane == 0, first, rest)


def unfold(pick, axis, u, v):
    mid = u.shape[axis] // 2
    part = (lambda x, i: x[i * mid : (i + 1) * mid]) if axis == 0 else (lambda x, i: x[:, i * mid : (i + 1) * mid])
    u1, u2, v1, v2 = part(u, 0), part(u, 1), part(v, 0), part(v, 1)
    real = jnp.concatenate([pick(u1, u1 + v2), pick(u2, u1 - v2)], axis=axis)
    imag = jnp.concatenate([pick(v1, v1 - u2), pick(v2, v1 + u2)], axis=axis)
    return real, imag


def fold(pick, axis, real, imag):
    mid = real.shape[axis] // 2
    part = (lambda x, i: x[i * mid : (i + 1) * mid]) if axis == 0 else (lambda x, i: x[:, i * mid : (i + 1) * mid])
    r1, r2, i1, i2 = part(real, 0), part(real, 1), part(imag, 0), part(imag, 1)
    a = jnp.concatenate([pick(r1, r1 + r2), pick(r2, i2 - i1)], axis=axis)
    b = jnp.concatenate([pick(i1, i1 + i2), pick(i2, r1 - r2)], axis=axis)
    return a.astype(BF16), b.astype(BF16)


def positions_kernel(
    tile_rows, pos_ref, where_ref, win_ref, probe_ref, meas_ref, right_ref, left_ref, *rest
):
    *out_refs, psum_ref, raw, obj, far, sums, grad, pacc = rest
    slots = win_ref.shape[0]
    per_holder = meas_ref.shape[0]
    modes = probe_ref.shape[1]
    patch = probe_ref.shape[2]
    both = 2 * tile_rows
    width = sums.shape[2]
    block_tiles = (patch + tile_rows - 1) // tile_rows + 1
    block_rows = block_tiles * tile_rows
    first_row = where_ref[slots]
    device = where_ref[slots + 1]
    tall = patch // SUBLANES
    sublane = lax.broadcasted_iota(jnp.int32, (tall + 1, SUBLANES, LANES), 1)
    lanes = lax.broadcasted_iota(jnp.int32, (patch, LANES), 1)
    cols = patch // LANES

    for t in range(slots):
        sums[t] = jnp.zeros(sums.shape[1:], BF16)
    pacc[...] = jnp.zeros(pacc.shape, F32)

    def visit(p, carry):
        tile, off, block, lane = place(
            pos_ref[0, p], pos_ref[1, p], first_row, tile_rows, slots, patch, width
        )
        sub = lax.rem(off, SUBLANES)
        base = pl.multiple_of(off - sub, SUBLANES)
        for j in range(block_tiles):
            for q in range(cols + 1):
                at = pl.ds(pl.multiple_of((block + q) * both, 16), both)
                part = win_ref[where_ref[tile + j], at, :].astype(F32)
                raw[0, q, j * tile_rows : (j + 1) * tile_rows] = part[:tile_rows]
                raw[1, q, j * tile_rows : (j + 1) * tile_rows] = part[tile_rows:]
        for c in range(2):
            turned = []
            for q in range(cols + 1):
                rows = raw[c, q, pl.ds(base, patch + SUBLANES), :].reshape(tall + 1, SUBLANES, LANES)
                rows = pltpu.roll(rows, lax.rem(SUBLANES - sub, SUBLANES), 1)
                rows = jnp.where(sublane[:tall] < SUBLANES - sub, rows[:tall], rows[1:])
                turned.append(pltpu.roll(rows.reshape(patch, LANES), lax.rem(LANES - lane, LANES), 1))
            for q in range(cols):
                obj[c, :, q * LANES : (q + 1) * LANES] = jnp.where(lanes < LANES - lane, turned[q], turned[q + 1])
        pacc[2 * modes] = pacc[2 * modes] + (obj[0] * obj[0] + obj[1] * obj[1])
        model = jnp.ones((patch, patch), F32)
        for m in range(modes):
            probe_real, probe_imag = probe_ref[0, m], probe_ref[1, m]
            exit_real = (probe_real * obj[0] - probe_imag * obj[1]).astype(BF16)
            exit_imag = (probe_real * obj[1] + probe_imag * obj[0]).astype(BF16)
            half_real, half_imag = unfold(
                with_first_lane, 1, dot(exit_real, right_ref[...]), dot(exit_imag, right_ref[...])
            )
            far_real, far_imag = unfold(
                with_first_row, 0, dot(left_ref[...], half_real.astype(BF16)), dot(left_ref[...], half_imag.astype(BF16))
            )
            far[0, m] = far_real
            far[1, m] = far_imag
            model = model + (far_real * far_real + far_imag * far_imag)
        factor = jnp.sqrt(meas_ref[p] / model) - 1.0
        grad_real = jnp.zeros((patch, patch), F32)
        grad_imag = jnp.zeros((patch, patch), F32)
        for m in range(modes):
            a, b = fold(with_first_lane, 1, far[0, m] * factor, far[1, m] * factor)
            a, b = fold(with_first_row, 0, dot(a, left_ref[...]), dot(b, left_ref[...]))
            change_real, change_imag = dot(right_ref[...], a), dot(right_ref[...], b)
            probe_real, probe_imag = probe_ref[0, m], probe_ref[1, m]
            grad_real = grad_real + (probe_real * change_real + probe_imag * change_imag)
            grad_imag = grad_imag + (probe_real * change_imag - probe_imag * change_real)
            pacc[m] = pacc[m] + (obj[0] * change_real + obj[1] * change_imag)
            pacc[modes + m] = pacc[modes + m] + (obj[0] * change_imag - obj[1] * change_real)
        edge = jnp.zeros((1, SUBLANES, LANES), F32)
        for c, value in enumerate((grad_real, grad_imag)):
            turned = [
                pltpu.roll(value[:, q * LANES : (q + 1) * LANES], lax.rem(lane, LANES), 1) for q in range(cols)
            ]
            for q in range(cols + 1):
                here = turned[q] if q < cols else jnp.zeros((patch, LANES), F32)
                before = turned[q - 1] if q > 0 else jnp.zeros((patch, LANES), F32)
                wide = jnp.where(lanes >= lane, here, before).reshape(tall, SUBLANES, LANES)
                wide = pltpu.roll(wide, sub, 1)
                wide = jnp.where(
                    sublane >= sub, jnp.concatenate([wide, edge], axis=0), jnp.concatenate([edge, wide], axis=0)
                )
                grad[c, q] = jnp.zeros(grad.shape[2:], F32)
                grad[c, q, pl.ds(base, patch + SUBLANES), :] = wide.reshape(patch + SUBLANES, LANES)
        for j in range(block_tiles):
            slot = where_ref[tile + j]
            rows = slice(j * tile_rows, (j + 1) * tile_rows)
            for q in range(cols + 1):
                at = pl.ds(pl.multiple_of((block + q) * LANES, LANES), LANES)
                part = jnp.concatenate([grad[0, q, rows], grad[1, q, rows]], axis=0)
                sums[slot, :, at] = (sums[slot, :, at].astype(F32) + part).astype(BF16)
        return carry

    lax.fori_loop(0, per_holder, visit, 0)

    for t in range(slots):
        out_refs[t][...] = sums[t]
    pieces = psum_ref.shape[0]
    rows = patch // pieces

    def hand_out_probe(s, carry):
        piece = piece_of(s, device)
        psum_ref[s] = pacc[:, pl.ds(pl.multiple_of(piece * rows, rows), rows), :].astype(BF16)
        return carry

    lax.fori_loop(0, pieces, hand_out_probe, 0)

def move(value, steps):
    count = lax.axis_size("tile")
    pairs = []
    for i in range(count):
        kind, step = steps[i % 2]
        if kind == "bit":
            to = i ^ step
        else:
            to = i + (step if (i // 2) % 2 == 0 else -step)
        if 0 <= to < count:
            pairs.append((i, to))
    return lax.ppermute(value, "tile", pairs)


def swap_bits(value, bit0, bit1):
    return move(value, (("bit", bit0), ("bit", bit1)))


def to_sibling(value):
    return swap_bits(value, 1, 1)


def piece_of(s, device):
    core = device & 1
    other = s >> (BITS - 1)
    mine = core ^ other
    away0 = sum(((s >> (BITS - 2 - j)) & 1) * bit for j, bit in enumerate(PROBE_BITS[0]))
    away1 = sum(((s >> (BITS - 2 - j)) & 1) * bit for j, bit in enumerate(PROBE_BITS[1]))
    return ((device & (2**BITS - 1)) ^ other) ^ jnp.where(mine == 0, away0, away1)


def place(row, col, first_row, tile_rows, window_tiles, patch, width):
    block_tiles = (patch + tile_rows - 1) // tile_rows + 1
    local_row = row - first_row
    tile = jnp.clip(local_row // tile_rows, 0, window_tiles - block_tiles)
    block = jnp.minimum(col // LANES, (width - patch - LANES) // LANES)
    return tile, local_row - tile * tile_rows, block, col - block * LANES


def pack_kernel(pos_ref, obj_ref, out_ref):
    tile_rows, width = obj_ref.shape[1:]
    both = 2 * tile_rows
    for q in range(width // LANES):
        part = obj_ref[:, :, q * LANES : (q + 1) * LANES].reshape(both, LANES)
        out_ref[q * both : (q + 1) * both] = part.astype(BF16)
    lane = lax.broadcasted_iota(jnp.int32, (HEAD_ROWS, LANES), 1)
    head = jnp.zeros((HEAD_ROWS, LANES), jnp.int32)
    for k in range(2 * pos_ref.shape[1]):
        value = pos_ref[k % 2, k // 2]
        head = jnp.where(lane == 2 * k, value // BASE, head)
        head = jnp.where(lane == 2 * k + 1, lax.rem(value, BASE), head)
    out_ref[width // LANES * both :] = head.astype(F32).astype(BF16)


def coverage_kernel(tile_rows, per_holder, index_ref, heads_ref, probe_ref, out_ref, padded, digits, pos_ref):
    modes, patch = probe_ref.shape[1], probe_ref.shape[2]
    width = out_ref.shape[1]
    slots = heads_ref.shape[0]
    me, count = index_ref[slots], index_ref[slots + 1]
    for s in range(slots):
        digits[s : s + 1] = heads_ref[s].astype(F32)[:1].astype(jnp.int32)
    pltpu.sync_copy(digits, pos_ref)
    total = jnp.zeros((patch, patch), F32)
    for m in range(modes):
        total = total + (probe_ref[0, m] * probe_ref[0, m] + probe_ref[1, m] * probe_ref[1, m])
    padded[...] = jnp.zeros(padded.shape, F32)
    for q in range(patch // LANES):
        padded[q, tile_rows : tile_rows + patch] = total[:, q * LANES : (q + 1) * LANES]
    sublane = lax.broadcasted_iota(jnp.int32, (tile_rows // SUBLANES, SUBLANES, LANES), 1)
    lanes = lax.broadcasted_iota(jnp.int32, (tile_rows, LANES), 1)
    out_ref[...] = jnp.ones(out_ref.shape, F32)

    def visit(k, carry):
        s, p = k // per_holder, lax.rem(k, per_holder)
        holder = index_ref[s]
        row = pos_ref[s, 4 * p] * BASE + pos_ref[s, 4 * p + 1]
        col = pos_ref[s, 4 * p + 2] * BASE + pos_ref[s, 4 * p + 3]
        at = me * tile_rows - row + tile_rows
        col_block = jnp.minimum(col // LANES, (width - patch - LANES) // LANES)
        there = jnp.logical_and(holder >= 0, holder < count)

        @pl.when(jnp.logical_and(there, jnp.logical_and(at > 0, at < tile_rows + patch)))
        def _():
            sub = lax.rem(at, SUBLANES)
            lane = col - col_block * LANES
            turned = []
            for q in range(patch // LANES):
                rows = padded[q, pl.ds(pl.multiple_of(at - sub, SUBLANES), tile_rows + SUBLANES), :]
                rows = pltpu.roll(rows.reshape(-1, SUBLANES, LANES), lax.rem(SUBLANES - sub, SUBLANES), 1)
                rows = jnp.where(sublane < SUBLANES - sub, rows[:-1], rows[1:]).reshape(tile_rows, LANES)
                turned.append(pltpu.roll(rows, lax.rem(lane, LANES), 1))
            for q in range(patch // LANES + 1):
                here = turned[q] if q < patch // LANES else jnp.zeros((tile_rows, LANES), F32)
                before = turned[q - 1] if q > 0 else jnp.zeros((tile_rows, LANES), F32)
                cols = pl.ds(pl.multiple_of((col_block + q) * LANES, LANES), LANES)
                out_ref[:, cols] = out_ref[:, cols] + jnp.where(lanes >= lane, here, before)

        return carry

    lax.fori_loop(0, slots * per_holder, visit, 0)


def order_kernel(order_ref, meas_ref, out_ref):
    turn = order_ref[...]
    for p in range(meas_ref.shape[0]):
        rows = jnp.dot(turn, meas_ref[p], preferred_element_type=F32, precision=lax.Precision.HIGHEST)
        out_ref[p] = lax.dot_general(
            rows, turn, (((1,), (1,)), ((), ())), preferred_element_type=F32, precision=lax.Precision.HIGHEST
        )


def unpack_kernel(index_ref, pieces_ref, out_ref):
    pieces, planes, rows, cols = pieces_ref.shape
    modes = out_ref.shape[1]
    device = index_ref[0]

    def visit(s, carry):
        piece = piece_of(s, device)
        at = pl.ds(pl.multiple_of(piece * rows, rows), rows)
        value = pieces_ref[s].astype(F32)
        for c in range(2):
            out_ref[c, :, at, :] = value[c * modes : (c + 1) * modes]
        return carry

    lax.fori_loop(0, pieces, visit, 0)


VMEM = pl.BlockSpec(memory_space=pltpu.VMEM)
SMEM = pl.BlockSpec(memory_space=pltpu.SMEM)


def call(kernel, name, out_shape, in_specs, limit, flops, bytes_accessed, scratch=()):
    return pl.pallas_call(
        kernel,
        out_shape=out_shape,
        in_specs=in_specs,
        out_specs=jax.tree.map(lambda _: VMEM, out_shape),
        scratch_shapes=list(scratch),
        compiler_params=pltpu.CompilerParams(vmem_limit_bytes=limit * MIB),
        cost_estimate=pl.CostEstimate(flops=flops, bytes_accessed=bytes_accessed, transcendentals=0),
        name=name,
    )


def add(a, b):
    return (a.astype(F32) + b.astype(F32)).astype(BF16)


def local(object_field, probe_modes, positions, intensity):
    tile_rows, width = object_field.shape[1:]
    modes, patch = probe_modes.shape[1:3]
    per_holder = positions.shape[0]
    count = lax.axis_size("tile")
    me = lax.axis_index("tile")
    core, chip = me % 2, me // 2
    block_rows = ((patch + tile_rows - 1) // tile_rows + 1) * tile_rows
    both = 2 * tile_rows
    tiles = 2 + 4 * REACH_CHIPS
    first_core = core == 0
    mine_first = positions.T

    own = call(
        pack_kernel, "pack", jax.ShapeDtypeStruct((width // LANES * both + HEAD_ROWS, LANES), BF16), [SMEM, VMEM],
        8, 1_000_000, 1_000_000,
    )(mine_first, object_field)
    pair = list(lax.optimization_barrier((own, to_sibling(own))))
    first = [move(v, (("shift", -4), ("bit", 2))) for v in pair]
    second = [move(jnp.where(first_core, u, v), (("bit", 2), ("shift", 4))) for u, v in zip(first, pair)]
    third = [move(jnp.where(first_core, u, v), (("shift", 4), ("shift", -4))) for u, v in zip(second, first)]
    brought = first + second + third
    window = pair + brought + [to_sibling(v) for v in brought]

    cases = []
    for c in range(2):
        slots = [(0, c), (0, 1 - c)]
        slots += [(away, t) for away in BROUGHT[c] for t in (c, 1 - c)]
        slots += [(away, t) for away in BROUGHT[1 - c] for t in (1 - c, c)]
        order = [(w // 2 - REACH_CHIPS, w % 2) for w in range(tiles)]
        cases.append(
            [
                np.array([away for away, _ in slots]),
                np.array([t for _, t in slots]),
                np.array([slots.index((away, t)) for away, t in order]),
                np.array([slots.index((-away, t)) for away, t in order]),
            ]
        )
    aways, cores, even_where, odd_where = [jnp.where(first_core, u, v) for u, v in zip(*cases, strict=True)]
    even = chip % 2 == 0
    holders = 2 * (chip + jnp.where(even, aways, -aways)) + cores
    index = jnp.concatenate([holders, me[None], jnp.full((1,), count)]).astype(jnp.int32)
    first_row = (2 * (chip - REACH_CHIPS)) * tile_rows
    where = jnp.concatenate([jnp.where(even, even_where, odd_where), first_row[None], me[None]]).astype(jnp.int32)

    right, left = real_tables(patch)
    ordered = call(
        order_kernel, "order", jax.ShapeDtypeStruct(intensity.shape, F32), [VMEM, VMEM], 8, 2_000_000_000, 2_000_000
    )(jnp.asarray(frequency_order(patch)), lax.optimization_barrier((intensity, first[0]))[0])

    pieces = 2**BITS
    rows = patch // pieces
    planes = 2 * modes + 1
    cols = patch // LANES
    *sums, psum = call(
        lambda *refs: positions_kernel(tile_rows, *refs), "positions",
        (jax.ShapeDtypeStruct((both, width), BF16),) * tiles + (jax.ShapeDtypeStruct((pieces, planes, rows, patch), BF16),),
        [SMEM, SMEM, VMEM, VMEM, VMEM, VMEM, VMEM],
        24, 10_000_000_000, 20_000_000,
        [
            pltpu.VMEM((2, cols + 1, block_rows + 16, LANES), F32),
            pltpu.VMEM((2, patch, patch), F32),
            pltpu.VMEM((2, modes, patch, patch), F32),
            pltpu.VMEM((tiles, both, width), BF16),
            pltpu.VMEM((2, cols + 1, block_rows + 16, LANES), F32),
            pltpu.VMEM((planes, patch, patch), F32),
        ],
    )(mine_first, where, jnp.stack(window), probe_modes, ordered, right, left)

    own_sum, sibling_sum, *sums = sums
    kept, given = sums[: 2 * REACH_CHIPS], sums[2 * REACH_CHIPS :]
    sums = [None] * 2 * REACH_CHIPS
    for j in (5, 4, 3, 2, 1, 0):
        sums[j] = add(kept[j], to_sibling(given[j]))
    came3 = [move(sums[4 + j], (("shift", -4), ("shift", 4))) for j in (1, 0)]
    sum2 = [add(sums[2 + j], jnp.where(first_core, v, 0)) for j, v in zip((1, 0), came3)]
    came2 = [move(v, (("bit", 2), ("shift", -4))) for v in sum2]
    sum1 = [add(sums[j], jnp.where(first_core, u, v)) for j, u, v in zip((1, 0), came2, came3)]
    came1 = [move(v, (("shift", 4), ("bit", 2))) for v in sum1]
    came = [u.astype(F32) + jnp.where(first_core, 0, v).astype(F32) for u, v in zip(came1, came2)]
    total = own_sum.astype(F32) + to_sibling((sibling_sum.astype(F32) + came[0]).astype(BF16)).astype(F32) + came[1]
    heads, _ = lax.optimization_barrier((jnp.stack([v[-HEAD_ROWS:] for v in window]), sums[5]))
    coverage = call(
        lambda *refs: coverage_kernel(tile_rows, per_holder, *refs), "coverage",
        jax.ShapeDtypeStruct((tile_rows, width), F32), [SMEM, VMEM, VMEM],
        8, 10_000_000, 3_000_000,
        [
            pltpu.VMEM((patch // LANES, patch + 2 * tile_rows + 16, LANES), F32),
            pltpu.VMEM((16, LANES), jnp.int32),
            pltpu.SMEM((16, LANES), jnp.int32),
        ],
    )(index, heads, probe_modes)

    object_step = total.reshape(2, tile_rows, width) / coverage[None]

    psum = psum.reshape((2,) * BITS + (planes, rows, patch))
    psum = add(psum[0], to_sibling(psum[1]))
    (a0, b0, c0), (a1, b1, c1) = PROBE_BITS
    psum = add(psum[0], swap_bits(psum[1], a0, a1))
    psum = add(psum[0], swap_bits(psum[1], b0, b1))
    psum = add(psum, swap_bits(psum, c0, c1)[::-1])
    bit = 1 << BITS
    while bit < count:
        psum = add(psum, swap_bits(psum, bit, bit))
        bit *= 2
    psum = psum.astype(F32)
    pstep = (psum[:, : 2 * modes] / jnp.sqrt(1.0 + psum[:, 2 * modes :])).astype(BF16)
    pstep = jnp.stack([pstep, swap_bits(pstep, b0, b1)])
    pstep = jnp.stack([pstep, swap_bits(pstep, a0, a1)])
    pstep = jnp.stack([pstep, to_sibling(pstep)])
    probe_step = call(
        unpack_kernel, "probe_unpack", jax.ShapeDtypeStruct(probe_modes.shape, F32), [SMEM, VMEM], 8, 1_000_000, 3_000_000
    )(me[None].astype(jnp.int32), pstep.reshape(pieces, 2 * modes, rows, patch))
    return (object_step, probe_step)


def solution(mesh):
    in_specs = (
        P(None, ("grp", "tile"), None),
        P(None, "grp", None, None),
        P(("grp", "tile"), None),
        P(("grp", "tile"), None, None),
    )
    out_specs = (P(None, ("grp", "tile"), None), P(None, "grp", None, None))
    return jax.shard_map(local, mesh=mesh, in_specs=in_specs, out_specs=out_specs, check_vma=False)
```

```python
import math

import jax
import jax.numpy as jnp
import numpy as np
from jax import lax
from jax.experimental import pallas as pl
from jax.experimental.pallas import tpu as pltpu
from jax.sharding import PartitionSpec as P

F32 = jnp.float32
BF16 = jnp.bfloat16
LANES = 128
SUBLANES = 8
MIB = 1024 * 1024
BROUGHT = ((2, -1, -3), (1, -2, 3))
REACH_CHIPS = 3
PROBE_BITS = ((2, 4, 8), (4, 8, 2))
BITS = 4
HEAD_ROWS = 16
BASE = 128
CHUNK = 32


def real_tables(size):
    steps = np.arange(size)
    phase = (steps[:, None] * steps[None, :] % size) * (2.0 * math.pi / size)
    factor = 1.0 / math.sqrt(size)
    cos_table, sine_table = np.cos(phase) * factor, np.sin(phase) * factor
    mid = size // 2
    table = np.concatenate([cos_table[:, :mid], cos_table[:, mid : mid + 1], sine_table[:, 1:mid]], axis=1)
    return jnp.asarray(table, BF16), jnp.asarray(table.T.copy(), BF16)


def frequency_order(size):
    mid = size // 2
    order = np.concatenate([np.arange(mid), [mid], np.arange(size - 1, mid, -1)])
    return np.eye(size, dtype=np.float32)[order]


def dot(a, b):
    return jnp.dot(a, b, preferred_element_type=F32)


def with_first_row(first, rest):
    row = lax.broadcasted_iota(jnp.int32, (SUBLANES, rest.shape[1]), 0)
    top = jnp.where(row == 0, first[:SUBLANES], rest[:SUBLANES])
    return jnp.concatenate([top, rest[SUBLANES:]], axis=0)


def with_first_lane(first, rest):
    lane = lax.broadcasted_iota(jnp.int32, rest.shape, 1)
    return jnp.where(lane == 0, first, rest)


def unfold(pick, axis, u, v):
    mid = u.shape[axis] // 2
    part = (lambda x, i: x[i * mid : (i + 1) * mid]) if axis == 0 else (lambda x, i: x[:, i * mid : (i + 1) * mid])
    u1, u2, v1, v2 = part(u, 0), part(u, 1), part(v, 0), part(v, 1)
    real = jnp.concatenate([pick(u1, u1 + v2), pick(u2, u1 - v2)], axis=axis)
    imag = jnp.concatenate([pick(v1, v1 - u2), pick(v2, v1 + u2)], axis=axis)
    return real, imag


def fold(pick, axis, real, imag):
    mid = real.shape[axis] // 2
    part = (lambda x, i: x[i * mid : (i + 1) * mid]) if axis == 0 else (lambda x, i: x[:, i * mid : (i + 1) * mid])
    r1, r2, i1, i2 = part(real, 0), part(real, 1), part(imag, 0), part(imag, 1)
    a = jnp.concatenate([pick(r1, r1 + r2), pick(r2, i2 - i1)], axis=axis)
    b = jnp.concatenate([pick(i1, i1 + i2), pick(i2, r1 - r2)], axis=axis)
    return a.astype(BF16), b.astype(BF16)


def positions_kernel(
    tile_rows, pos_ref, where_ref, win_ref, probe_ref, meas_ref, right_ref, left_ref,
    grad_ref, psum_ref, raw, obj, far, half, pacc,
):
    slots = win_ref.shape[0]
    per_holder = meas_ref.shape[0]
    modes = probe_ref.shape[1]
    patch = probe_ref.shape[2]
    both = 2 * tile_rows
    width = win_ref.shape[1] // both * LANES
    block_tiles = (patch + tile_rows - 1) // tile_rows + 1
    first_row = where_ref[slots]
    device = where_ref[slots + 1]
    tall = patch // SUBLANES
    sublane = lax.broadcasted_iota(jnp.int32, (tall, SUBLANES, LANES), 1)
    lanes = lax.broadcasted_iota(jnp.int32, (patch, LANES), 1)
    cols = patch // LANES
    pacc[...] = jnp.zeros(pacc.shape, F32)

    def visit(p, carry):
        tile, off, block, lane = place(
            pos_ref[0, p], pos_ref[1, p], first_row, tile_rows, slots, patch, width
        )
        sub = lax.rem(off, SUBLANES)
        base = pl.multiple_of(off - sub, SUBLANES)
        for j in range(block_tiles):
            for q in range(cols + 1):
                at = pl.ds(pl.multiple_of((block + q) * both, 16), both)
                part = win_ref[where_ref[tile + j], at, :].astype(F32)
                raw[0, q, j * tile_rows : (j + 1) * tile_rows] = part[:tile_rows]
                raw[1, q, j * tile_rows : (j + 1) * tile_rows] = part[tile_rows:]
        for c in range(2):
            turned = []
            for q in range(cols + 1):
                rows = raw[c, q, pl.ds(base, patch + SUBLANES), :].reshape(tall + 1, SUBLANES, LANES)
                rows = pltpu.roll(rows, lax.rem(SUBLANES - sub, SUBLANES), 1)
                rows = jnp.where(sublane < SUBLANES - sub, rows[:tall], rows[1:])
                turned.append(pltpu.roll(rows.reshape(patch, LANES), lax.rem(LANES - lane, LANES), 1))
            for q in range(cols):
                obj[c, :, q * LANES : (q + 1) * LANES] = jnp.where(lanes < LANES - lane, turned[q], turned[q + 1])
        pacc[2 * modes] = pacc[2 * modes] + (obj[0] * obj[0] + obj[1] * obj[1])
        for i in range(patch // CHUNK):
            at = slice(i * CHUNK, (i + 1) * CHUNK)
            obj_real, obj_imag = obj[0, at, :], obj[1, at, :]
            exits = []
            for m in range(modes):
                probe_real, probe_imag = probe_ref[0, m, at, :], probe_ref[1, m, at, :]
                exits.append((probe_real * obj_real - probe_imag * obj_imag).astype(BF16))
                exits.append((probe_real * obj_imag + probe_imag * obj_real).astype(BF16))
            out = dot(jnp.concatenate(exits, axis=0), right_ref[...])
            for m in range(modes):
                u, v = [out[(2 * m + j) * CHUNK : (2 * m + j + 1) * CHUNK] for j in range(2)]
                real, imag = unfold(with_first_lane, 1, u, v)
                half[m, at, :patch] = real.astype(BF16)
                half[m, at, patch:] = imag.astype(BF16)
        for m in range(modes):
            out = dot(left_ref[...], half[m])
            far[0, m], far[1, m] = unfold(with_first_row, 0, out[:, :patch], out[:, patch:])
        mid = patch // 2

        def both_halves(ref, lead, start, cols=slice(None)):
            low, high = [ref[(*lead, slice(at, at + CHUNK // 2), cols)] for at in (start, start + mid)]
            return jnp.concatenate([low, high], axis=0)

        for start in range(0, mid, CHUNK // 2):
            fars = [(both_halves(far, (0, m), start), both_halves(far, (1, m), start)) for m in range(modes)]
            model = 1.0 + sum(r * r + i * i for r, i in fars)
            factor = both_halves(meas_ref, (p,), start) * lax.rsqrt(model) - 1.0
            folded = []
            for r, i in fars:
                folded += fold(with_first_lane, 1, r * factor, i * factor)
            out = dot(jnp.concatenate(folded, axis=0), left_ref[...])

            pick = with_first_row if start == 0 else lambda top, rest: rest
            low, high = slice(start, start + CHUNK // 2), slice(start + mid, start + mid + CHUNK // 2)
            for m in range(modes):
                u, v = [out[(2 * m + j) * CHUNK : (2 * m + j + 1) * CHUNK] for j in range(2)]
                for part, side in zip(fold(pick, 0, u, v), (slice(0, patch), slice(patch, None)), strict=True):
                    half[m, low, side], half[m, high, side] = part[: CHUNK // 2], part[CHUNK // 2 :]
        for m in range(modes):
            out = dot(right_ref[...], half[m])
            far[0, m] = out[:, :patch]
            far[1, m] = out[:, patch:]

        for i in range(patch // CHUNK):
            at = slice(i * CHUNK, (i + 1) * CHUNK)
            obj_real, obj_imag = obj[0, at, :], obj[1, at, :]
            grad_real = jnp.zeros((CHUNK, patch), F32)
            grad_imag = jnp.zeros((CHUNK, patch), F32)
            for m in range(modes):
                change_real, change_imag = far[0, m, at, :], far[1, m, at, :]
                probe_real, probe_imag = probe_ref[0, m, at, :], probe_ref[1, m, at, :]
                grad_real = grad_real + (probe_real * change_real + probe_imag * change_imag)
                grad_imag = grad_imag + (probe_real * change_imag - probe_imag * change_real)
                pacc[m, at, :] = pacc[m, at, :] + (obj_real * change_real + obj_imag * change_imag)
                pacc[modes + m, at, :] = pacc[modes + m, at, :] + (obj_real * change_imag - obj_imag * change_real)
            grad_ref[p, 0, at, :] = grad_real
            grad_ref[p, 1, at, :] = grad_imag
        return carry

    lax.fori_loop(0, per_holder, visit, 0)

    pieces = psum_ref.shape[0]
    rows = patch // pieces

    def hand_out_probe(s, carry):
        piece = piece_of(s, device)
        psum_ref[s] = pacc[:, pl.ds(pl.multiple_of(piece * rows, rows), rows), :].astype(BF16)
        return carry

    lax.fori_loop(0, pieces, hand_out_probe, 0)

def place_kernel(tile_rows, pos_ref, where_ref, grad_ref, *rest):
    *out_refs, sums, grad = rest
    slots = len(out_refs)
    per_holder, _, patch, _ = grad_ref.shape
    width = sums.shape[2]
    block_tiles = (patch + tile_rows - 1) // tile_rows + 1
    first_row = where_ref[slots]
    tall = patch // SUBLANES
    sublane = lax.broadcasted_iota(jnp.int32, (tall + 1, SUBLANES, LANES), 1)
    lanes = lax.broadcasted_iota(jnp.int32, (patch, LANES), 1)
    cols = patch // LANES
    edge = jnp.zeros((1, SUBLANES, LANES), F32)
    for t in range(slots):
        sums[t] = jnp.zeros(sums.shape[1:], BF16)

    def visit(p, carry):
        tile, off, block, lane = place(
            pos_ref[0, p], pos_ref[1, p], first_row, tile_rows, slots, patch, width
        )
        sub = lax.rem(off, SUBLANES)
        base = pl.multiple_of(off - sub, SUBLANES)
        for c in range(2):
            turned = [
                pltpu.roll(grad_ref[p, c, :, q * LANES : (q + 1) * LANES], lax.rem(lane, LANES), 1) for q in range(cols)
            ]
            for q in range(cols + 1):
                here = turned[q] if q < cols else jnp.zeros((patch, LANES), F32)
                before = turned[q - 1] if q > 0 else jnp.zeros((patch, LANES), F32)
                wide = jnp.where(lanes >= lane, here, before).reshape(tall, SUBLANES, LANES)
                wide = pltpu.roll(wide, sub, 1)
                wide = jnp.where(
                    sublane >= sub, jnp.concatenate([wide, edge], axis=0), jnp.concatenate([edge, wide], axis=0)
                )
                grad[c, q] = jnp.zeros(grad.shape[2:], F32)
                grad[c, q, pl.ds(base, patch + SUBLANES), :] = wide.reshape(patch + SUBLANES, LANES)
        for j in range(block_tiles):
            slot = where_ref[tile + j]
            rows = slice(j * tile_rows, (j + 1) * tile_rows)
            for q in range(cols + 1):
                at = pl.ds(pl.multiple_of((block + q) * LANES, LANES), LANES)
                part = jnp.concatenate([grad[0, q, rows], grad[1, q, rows]], axis=0)
                sums[slot, :, at] = (sums[slot, :, at].astype(F32) + part).astype(BF16)
        return carry

    lax.fori_loop(0, per_holder, visit, 0)

    for t in range(slots):
        out_refs[t][...] = sums[t]


def move(value, steps):
    count = lax.axis_size("tile")
    pairs = []
    for i in range(count):
        kind, step = steps[i % 2]
        if kind == "bit":
            to = i ^ step
        else:
            to = i + (step if (i // 2) % 2 == 0 else -step)
        if 0 <= to < count:
            pairs.append((i, to))
    return lax.ppermute(value, "tile", pairs)


def swap_bits(value, bit0, bit1):
    return move(value, (("bit", bit0), ("bit", bit1)))


def to_sibling(value):
    return swap_bits(value, 1, 1)


def piece_of(s, device):
    core = device & 1
    other = s >> (BITS - 1)
    mine = core ^ other
    away0 = sum(((s >> (BITS - 2 - j)) & 1) * bit for j, bit in enumerate(PROBE_BITS[0]))
    away1 = sum(((s >> (BITS - 2 - j)) & 1) * bit for j, bit in enumerate(PROBE_BITS[1]))
    return ((device & (2**BITS - 1)) ^ other) ^ jnp.where(mine == 0, away0, away1)


def place(row, col, first_row, tile_rows, window_tiles, patch, width):
    block_tiles = (patch + tile_rows - 1) // tile_rows + 1
    local_row = row - first_row
    tile = jnp.clip(local_row // tile_rows, 0, window_tiles - block_tiles)
    block = jnp.minimum(col // LANES, (width - patch - LANES) // LANES)
    return tile, local_row - tile * tile_rows, block, col - block * LANES


def pack_kernel(pos_ref, obj_ref, out_ref):
    tile_rows, width = obj_ref.shape[1:]
    both = 2 * tile_rows
    for q in range(width // LANES):
        part = obj_ref[:, :, q * LANES : (q + 1) * LANES].reshape(both, LANES)
        out_ref[q * both : (q + 1) * both] = part.astype(BF16)
    lane = lax.broadcasted_iota(jnp.int32, (HEAD_ROWS, LANES), 1)
    head = jnp.zeros((HEAD_ROWS, LANES), jnp.int32)
    for k in range(2 * pos_ref.shape[1]):
        value = pos_ref[k % 2, k // 2]
        head = jnp.where(lane == 2 * k, value // BASE, head)
        head = jnp.where(lane == 2 * k + 1, lax.rem(value, BASE), head)
    out_ref[width // LANES * both :] = head.astype(F32).astype(BF16)


def coverage_kernel(tile_rows, per_holder, index_ref, heads_ref, probe_ref, out_ref, padded, digits, pos_ref):
    modes, patch = probe_ref.shape[1], probe_ref.shape[2]
    width = out_ref.shape[1]
    slots = heads_ref.shape[0]
    me, count = index_ref[slots], index_ref[slots + 1]
    for s in range(slots):
        digits[s : s + 1] = heads_ref[s].astype(F32)[:1].astype(jnp.int32)
    pltpu.sync_copy(digits, pos_ref)
    total = jnp.zeros((patch, patch), F32)
    for m in range(modes):
        total = total + (probe_ref[0, m] * probe_ref[0, m] + probe_ref[1, m] * probe_ref[1, m])
    padded[...] = jnp.zeros(padded.shape, F32)
    for q in range(patch // LANES):
        padded[q, tile_rows : tile_rows + patch] = total[:, q * LANES : (q + 1) * LANES]
    sublane = lax.broadcasted_iota(jnp.int32, (tile_rows // SUBLANES, SUBLANES, LANES), 1)
    lanes = lax.broadcasted_iota(jnp.int32, (tile_rows, LANES), 1)
    out_ref[...] = jnp.ones(out_ref.shape, F32)

    def shifted(s, p):
        row = pos_ref[s, 4 * p] * BASE + pos_ref[s, 4 * p + 1]
        col = pos_ref[s, 4 * p + 2] * BASE + pos_ref[s, 4 * p + 3]
        holder = index_ref[s]
        there = jnp.logical_and(holder >= 0, holder < count)
        at = jnp.where(there, jnp.clip(me * tile_rows - row + tile_rows, 0, tile_rows + patch), 0)
        block = jnp.minimum(col // LANES, (width - patch - LANES) // LANES)
        lane = col - block * LANES
        sub = lax.rem(at, SUBLANES)
        turned = []
        for q in range(patch // LANES):
            rows = padded[q, pl.ds(pl.multiple_of(at - sub, SUBLANES), tile_rows + SUBLANES), :]
            rows = pltpu.roll(rows.reshape(-1, SUBLANES, LANES), lax.rem(SUBLANES - sub, SUBLANES), 1)
            rows = jnp.where(sublane < SUBLANES - sub, rows[:-1], rows[1:]).reshape(tile_rows, LANES)
            turned.append(pltpu.roll(rows, lax.rem(lane, LANES), 1))
        zero = jnp.zeros((tile_rows, LANES), F32)
        parts = [jnp.where(lanes >= lane, u, v) for u, v in zip(turned + [zero], [zero] + turned)]
        return block, parts

    def visit(s, carry):
        for block, parts in [shifted(s, p) for p in range(per_holder)]:
            for q, part in enumerate(parts):
                cols = pl.ds(pl.multiple_of((block + q) * LANES, LANES), LANES)
                out_ref[:, cols] = out_ref[:, cols] + part
        return carry

    lax.fori_loop(0, slots, visit, 0)


def order_kernel(order_ref, meas_ref, out_ref):
    turn = order_ref[...]
    for p in range(meas_ref.shape[0]):
        rows = jnp.dot(turn, meas_ref[p], preferred_element_type=F32, precision=lax.Precision.HIGHEST)
        turned = lax.dot_general(
            rows, turn, (((1,), (1,)), ((), ())), preferred_element_type=F32, precision=lax.Precision.HIGHEST
        )
        out_ref[p] = jnp.sqrt(turned)


def finish_kernel(own_ref, sibling_ref, came_ref, coverage_ref, out_ref):
    rows = coverage_ref.shape[0]
    inverse = 1.0 / coverage_ref[...]
    for c in range(2):
        at = slice(c * rows, (c + 1) * rows)
        total = own_ref[...].astype(F32)[at] + sibling_ref[...].astype(F32)[at] + came_ref[at]
        out_ref[c] = total * inverse


def unpack_kernel(index_ref, pieces_ref, out_ref):
    pieces, planes, rows, cols = pieces_ref.shape
    modes = out_ref.shape[1]
    device = index_ref[0]

    def visit(s, carry):
        piece = piece_of(s, device)
        at = pl.ds(pl.multiple_of(piece * rows, rows), rows)
        value = pieces_ref[s].astype(F32)
        for c in range(2):
            out_ref[c, :, at, :] = value[c * modes : (c + 1) * modes]
        return carry

    lax.fori_loop(0, pieces, visit, 0)


VMEM = pl.BlockSpec(memory_space=pltpu.VMEM)
SMEM = pl.BlockSpec(memory_space=pltpu.SMEM)


def call(kernel, name, out_shape, in_specs, limit, flops, bytes_accessed, scratch=()):
    return pl.pallas_call(
        kernel,
        out_shape=out_shape,
        in_specs=in_specs,
        out_specs=jax.tree.map(lambda _: VMEM, out_shape),
        scratch_shapes=list(scratch),
        compiler_params=pltpu.CompilerParams(vmem_limit_bytes=limit * MIB),
        cost_estimate=pl.CostEstimate(flops=flops, bytes_accessed=bytes_accessed, transcendentals=0),
        name=name,
    )


def add(a, b):
    return (a.astype(F32) + b.astype(F32)).astype(BF16)


def local(object_field, probe_modes, positions, intensity):
    tile_rows, width = object_field.shape[1:]
    modes, patch = probe_modes.shape[1:3]
    per_holder = positions.shape[0]
    count = lax.axis_size("tile")
    me = lax.axis_index("tile")
    core, chip = me % 2, me // 2
    block_rows = ((patch + tile_rows - 1) // tile_rows + 1) * tile_rows
    both = 2 * tile_rows
    tiles = 2 + 4 * REACH_CHIPS
    first_core = core == 0
    mine_first = positions.T

    own = call(
        pack_kernel, "pack", jax.ShapeDtypeStruct((width // LANES * both + HEAD_ROWS, LANES), BF16), [SMEM, VMEM],
        8, 1_000_000, 1_000_000,
    )(mine_first, object_field)
    pair = list(lax.optimization_barrier((own, to_sibling(own))))
    first = [move(v, (("shift", -4), ("bit", 2))) for v in pair]
    second = [move(jnp.where(first_core, u, v), (("bit", 2), ("shift", 4))) for u, v in zip(first, pair)]
    third = [move(jnp.where(first_core, u, v), (("shift", 4), ("shift", -4))) for u, v in zip(second, first)]
    brought = first + second + third
    window = pair + brought + [to_sibling(v) for v in brought]

    cases = []
    for c in range(2):
        slots = [(0, c), (0, 1 - c)]
        slots += [(away, t) for away in BROUGHT[c] for t in (c, 1 - c)]
        slots += [(away, t) for away in BROUGHT[1 - c] for t in (1 - c, c)]
        order = [(w // 2 - REACH_CHIPS, w % 2) for w in range(tiles)]
        cases.append(
            [
                np.array([away for away, _ in slots]),
                np.array([t for _, t in slots]),
                np.array([slots.index((away, t)) for away, t in order]),
                np.array([slots.index((-away, t)) for away, t in order]),
            ]
        )
    aways, cores, even_where, odd_where = [jnp.where(first_core, u, v) for u, v in zip(*cases, strict=True)]
    even = chip % 2 == 0
    holders = 2 * (chip + jnp.where(even, aways, -aways)) + cores
    index = jnp.concatenate([holders, me[None], jnp.full((1,), count)]).astype(jnp.int32)
    first_row = (2 * (chip - REACH_CHIPS)) * tile_rows
    where = jnp.concatenate([jnp.where(even, even_where, odd_where), first_row[None], me[None]]).astype(jnp.int32)

    right, left = real_tables(patch)
    ordered = call(
        order_kernel, "order", jax.ShapeDtypeStruct(intensity.shape, F32), [VMEM, VMEM], 8, 2_000_000_000, 2_000_000
    )(jnp.asarray(frequency_order(patch)), lax.optimization_barrier((intensity, first[0]))[0])

    pieces = 2**BITS
    rows = patch // pieces
    planes = 2 * modes + 1
    cols = patch // LANES
    grads, psum = call(
        lambda *refs: positions_kernel(tile_rows, *refs), "positions",
        (
            jax.ShapeDtypeStruct((per_holder, 2, patch, patch), F32),
            jax.ShapeDtypeStruct((pieces, planes, rows, patch), BF16),
        ),
        [SMEM, SMEM, VMEM, VMEM, VMEM, VMEM, VMEM],
        16, 10_000_000_000, 12_000_000,
        [
            pltpu.VMEM((2, cols + 1, block_rows + 16, LANES), F32),
            pltpu.VMEM((2, patch, patch), F32),
            pltpu.VMEM((2, modes, patch, patch), F32),
            pltpu.VMEM((modes, patch, 2 * patch), BF16),
            pltpu.VMEM((planes, patch, patch), F32),
        ],
    )(mine_first, where, jnp.stack(window), probe_modes, ordered, right, left)
    (a0, b0, c0), (a1, b1, c1) = PROBE_BITS
    psum = psum.reshape((2,) * BITS + (planes, rows, patch))
    psum = add(psum[0], to_sibling(psum[1]))
    psum_came = swap_bits(psum[1], a0, a1)
    grads = lax.optimization_barrier((grads, psum))[0]
    sums = call(
        lambda *refs: place_kernel(tile_rows, *refs), "place",
        (jax.ShapeDtypeStruct((both, width), BF16),) * tiles,
        [SMEM, SMEM, VMEM],
        16, 1_000_000_000, 12_000_000,
        [
            pltpu.VMEM((tiles, both, width), BF16),
            pltpu.VMEM((2, cols + 1, block_rows + 16, LANES), F32),
        ],
    )(mine_first, where, grads)

    own_sum, sibling_sum, *sums = sums
    kept, given = sums[: 2 * REACH_CHIPS], list(sums[2 * REACH_CHIPS :])
    sums = [None] * 2 * REACH_CHIPS
    for j in (5, 4, 3, 2, 1, 0):
        if j < 4:
            given[j] = lax.optimization_barrier((given[j], sums[j + 2]))[0]
        sums[j] = add(kept[j], to_sibling(given[j]))
    psum = add(psum[0], psum_came)
    sums[5], sums[4], psum = lax.optimization_barrier((sums[5], sums[4], psum))
    heads, _ = lax.optimization_barrier((jnp.stack([v[-HEAD_ROWS:] for v in window]), sums[5]))
    coverage = call(
        lambda *refs: coverage_kernel(tile_rows, per_holder, *refs), "coverage",
        jax.ShapeDtypeStruct((tile_rows, width), F32), [SMEM, VMEM, VMEM],
        8, 10_000_000, 3_000_000,
        [
            pltpu.VMEM((patch // LANES, patch + 2 * tile_rows + 16, LANES), F32),
            pltpu.VMEM((16, LANES), jnp.int32),
            pltpu.SMEM((16, LANES), jnp.int32),
        ],
    )(index, heads, probe_modes)

    came3 = [move(sums[4 + j], (("shift", -4), ("shift", 4))) for j in (1, 0)]
    sum2 = [add(sums[2 + j], jnp.where(first_core, v, 0)) for j, v in zip((1, 0), came3)]
    came2 = [move(v, (("bit", 2), ("shift", -4))) for v in sum2]
    sum1 = [add(sums[j], jnp.where(first_core, u, v)) for j, u, v in zip((1, 0), came2, came3)]
    came1 = [move(v, (("shift", 4), ("bit", 2))) for v in sum1]
    came = [u.astype(F32) + jnp.where(first_core, 0, v).astype(F32) for u, v in zip(came1, came2)]
    from_sibling = to_sibling((sibling_sum.astype(F32) + came[0]).astype(BF16))
    object_step = call(
        finish_kernel, "finish", jax.ShapeDtypeStruct(object_field.shape, F32), [VMEM] * 4, 8, 1_000_000, 3_000_000
    )(own_sum, from_sibling, came[1], coverage)

    def after(value, *others):
        return lax.optimization_barrier((value, *others))[0]

    psum = add(psum[0], swap_bits(psum[1], b0, b1))
    psum = after(psum, came3[0], coverage)
    psum = add(psum, swap_bits(psum, c0, c1)[::-1])
    bit = 1 << BITS
    while bit < count:
        psum = add(psum, swap_bits(psum, bit, bit))
        bit *= 2
    psum = psum.astype(F32)
    pstep = (psum[:, : 2 * modes] / jnp.sqrt(1.0 + psum[:, 2 * modes :])).astype(BF16)
    pstep = after(pstep, came3[1])
    pstep = jnp.stack([pstep, swap_bits(pstep, b0, b1)])
    pstep = after(pstep, came2[1])
    pstep = jnp.stack([pstep, swap_bits(pstep, a0, a1)])
    pstep = jnp.stack([pstep, to_sibling(pstep)])
    probe_step = call(
        unpack_kernel, "probe_unpack", jax.ShapeDtypeStruct(probe_modes.shape, F32), [SMEM, VMEM], 8, 1_000_000, 3_000_000
    )(me[None].astype(jnp.int32), pstep.reshape(pieces, 2 * modes, rows, patch))
    return (object_step, probe_step)


def solution(mesh):
    in_specs = (
        P(None, ("grp", "tile"), None),
        P(None, "grp", None, None),
        P(("grp", "tile"), None),
        P(("grp", "tile"), None, None),
    )
    out_specs = (P(None, ("grp", "tile"), None), P(None, "grp", None, None))
    return jax.shard_map(local, mesh=mesh, in_specs=in_specs, out_specs=out_specs, check_vma=False)
```

```python
import math

import jax
import jax.numpy as jnp
import numpy as np
from jax import lax
from jax.experimental import pallas as pl
from jax.experimental.pallas import tpu as pltpu
from jax.sharding import PartitionSpec as P

F32 = jnp.float32
BF16 = jnp.bfloat16
LANES = 128
SUBLANES = 8
MIB = 1024 * 1024
BROUGHT = ((2, -1, -3), (1, -2, 3))
REACH_CHIPS = 3
PROBE_BITS = ((2, 4, 8), (4, 8, 2))
BITS = 4
HEAD_ROWS = 16
BASE = 128
CHUNK = 32


def real_tables(size):
    steps = np.arange(size)
    phase = (steps[:, None] * steps[None, :] % size) * (2.0 * math.pi / size)
    factor = 1.0 / math.sqrt(size)
    cos_table, sine_table = np.cos(phase) * factor, np.sin(phase) * factor
    mid = size // 2
    table = np.concatenate([cos_table[:, :mid], cos_table[:, mid : mid + 1], sine_table[:, 1:mid]], axis=1)
    return jnp.asarray(table, BF16), jnp.asarray(table.T.copy(), BF16)


def frequency_order(size):
    mid = size // 2
    order = np.concatenate([np.arange(mid), [mid], np.arange(size - 1, mid, -1)])
    return np.eye(size, dtype=np.float32)[order]


def dot(a, b):
    return jnp.dot(a, b, preferred_element_type=F32)


def with_first_row(first, rest):
    row = lax.broadcasted_iota(jnp.int32, (SUBLANES, rest.shape[1]), 0)
    top = jnp.where(row == 0, first[:SUBLANES], rest[:SUBLANES])
    return jnp.concatenate([top, rest[SUBLANES:]], axis=0)


def with_first_lane(first, rest):
    lane = lax.broadcasted_iota(jnp.int32, rest.shape, 1)
    return jnp.where(lane == 0, first, rest)


def unfold(pick, axis, u, v):
    mid = u.shape[axis] // 2
    part = (lambda x, i: x[i * mid : (i + 1) * mid]) if axis == 0 else (lambda x, i: x[:, i * mid : (i + 1) * mid])
    u1, u2, v1, v2 = part(u, 0), part(u, 1), part(v, 0), part(v, 1)
    real = jnp.concatenate([pick(u1, u1 + v2), pick(u2, u1 - v2)], axis=axis)
    imag = jnp.concatenate([pick(v1, v1 - u2), pick(v2, v1 + u2)], axis=axis)
    return real, imag


def fold(pick, axis, real, imag):
    mid = real.shape[axis] // 2
    part = (lambda x, i: x[i * mid : (i + 1) * mid]) if axis == 0 else (lambda x, i: x[:, i * mid : (i + 1) * mid])
    r1, r2, i1, i2 = part(real, 0), part(real, 1), part(imag, 0), part(imag, 1)
    a = jnp.concatenate([pick(r1, r1 + r2), pick(r2, i2 - i1)], axis=axis)
    b = jnp.concatenate([pick(i1, i1 + i2), pick(i2, r1 - r2)], axis=axis)
    return a.astype(BF16), b.astype(BF16)


def positions_kernel(
    tile_rows, pos_ref, where_ref, win_ref, probe_ref, meas_ref, right_ref, left_ref,
    grad_ref, psum_ref, raw, obj, far, half, pacc,
):
    slots = win_ref.shape[0]
    per_holder = meas_ref.shape[0]
    modes = probe_ref.shape[1]
    patch = probe_ref.shape[2]
    both = 2 * tile_rows
    width = win_ref.shape[1] // both * LANES
    block_tiles = (patch + tile_rows - 1) // tile_rows + 1
    first_row = where_ref[slots]
    device = where_ref[slots + 1]
    tall = patch // SUBLANES
    sublane = lax.broadcasted_iota(jnp.int32, (tall, SUBLANES, LANES), 1)
    lanes = lax.broadcasted_iota(jnp.int32, (patch, LANES), 1)
    cols = patch // LANES
    pacc[...] = jnp.zeros(pacc.shape, F32)

    def visit(p, carry):
        tile, off, block, lane = place(
            pos_ref[0, p], pos_ref[1, p], first_row, tile_rows, slots, patch, width
        )
        sub = lax.rem(off, SUBLANES)
        base = pl.multiple_of(off - sub, SUBLANES)
        for j in range(block_tiles):
            for q in range(cols + 1):
                at = pl.ds(pl.multiple_of((block + q) * both, 16), both)
                part = win_ref[where_ref[tile + j], at, :].astype(F32)
                raw[0, q, j * tile_rows : (j + 1) * tile_rows] = part[:tile_rows]
                raw[1, q, j * tile_rows : (j + 1) * tile_rows] = part[tile_rows:]
        for c in range(2):
            turned = []
            for q in range(cols + 1):
                rows = raw[c, q, pl.ds(base, patch + SUBLANES), :].reshape(tall + 1, SUBLANES, LANES)
                rows = pltpu.roll(rows, lax.rem(SUBLANES - sub, SUBLANES), 1)
                rows = jnp.where(sublane < SUBLANES - sub, rows[:tall], rows[1:])
                turned.append(pltpu.roll(rows.reshape(patch, LANES), lax.rem(LANES - lane, LANES), 1))
            for q in range(cols):
                obj[c, :, q * LANES : (q + 1) * LANES] = jnp.where(lanes < LANES - lane, turned[q], turned[q + 1])
        pacc[2 * modes] = pacc[2 * modes] + (obj[0] * obj[0] + obj[1] * obj[1])
        for i in range(patch // CHUNK):
            at = slice(i * CHUNK, (i + 1) * CHUNK)
            obj_real, obj_imag = obj[0, at, :], obj[1, at, :]
            exits = []
            for m in range(modes):
                probe_real, probe_imag = probe_ref[0, m, at, :], probe_ref[1, m, at, :]
                exits.append((probe_real * obj_real - probe_imag * obj_imag).astype(BF16))
                exits.append((probe_real * obj_imag + probe_imag * obj_real).astype(BF16))
            out = dot(jnp.concatenate(exits, axis=0), right_ref[...])
            for m in range(modes):
                u, v = [out[(2 * m + j) * CHUNK : (2 * m + j + 1) * CHUNK] for j in range(2)]
                real, imag = unfold(with_first_lane, 1, u, v)
                half[m, at, :patch] = real.astype(BF16)
                half[m, at, patch:] = imag.astype(BF16)
        for m in range(modes):
            out = dot(left_ref[...], half[m])
            far[0, m], far[1, m] = unfold(with_first_row, 0, out[:, :patch], out[:, patch:])
        mid = patch // 2

        def both_halves(ref, lead, start, cols=slice(None)):
            low, high = [ref[(*lead, slice(at, at + CHUNK // 2), cols)] for at in (start, start + mid)]
            return jnp.concatenate([low, high], axis=0)

        for start in range(0, mid, CHUNK // 2):
            fars = [(both_halves(far, (0, m), start), both_halves(far, (1, m), start)) for m in range(modes)]
            model = 1.0 + sum(r * r + i * i for r, i in fars)
            factor = both_halves(meas_ref, (p,), start) * lax.rsqrt(model) - 1.0
            folded = []
            for r, i in fars:
                folded += fold(with_first_lane, 1, r * factor, i * factor)
            out = dot(jnp.concatenate(folded, axis=0), left_ref[...])

            pick = with_first_row if start == 0 else lambda top, rest: rest
            low, high = slice(start, start + CHUNK // 2), slice(start + mid, start + mid + CHUNK // 2)
            for m in range(modes):
                u, v = [out[(2 * m + j) * CHUNK : (2 * m + j + 1) * CHUNK] for j in range(2)]
                for part, side in zip(fold(pick, 0, u, v), (slice(0, patch), slice(patch, None)), strict=True):
                    half[m, low, side], half[m, high, side] = part[: CHUNK // 2], part[CHUNK // 2 :]
        for m in range(modes):
            out = dot(right_ref[...], half[m])
            far[0, m] = out[:, :patch]
            far[1, m] = out[:, patch:]

        for i in range(patch // CHUNK):
            at = slice(i * CHUNK, (i + 1) * CHUNK)
            obj_real, obj_imag = obj[0, at, :], obj[1, at, :]
            grad_real = jnp.zeros((CHUNK, patch), F32)
            grad_imag = jnp.zeros((CHUNK, patch), F32)
            for m in range(modes):
                change_real, change_imag = far[0, m, at, :], far[1, m, at, :]
                probe_real, probe_imag = probe_ref[0, m, at, :], probe_ref[1, m, at, :]
                grad_real = grad_real + (probe_real * change_real + probe_imag * change_imag)
                grad_imag = grad_imag + (probe_real * change_imag - probe_imag * change_real)
                pacc[m, at, :] = pacc[m, at, :] + (obj_real * change_real + obj_imag * change_imag)
                pacc[modes + m, at, :] = pacc[modes + m, at, :] + (obj_real * change_imag - obj_imag * change_real)
            grad_ref[p, 0, at, :] = grad_real
            grad_ref[p, 1, at, :] = grad_imag
        return carry

    lax.fori_loop(0, per_holder, visit, 0)

    pieces = psum_ref.shape[0]
    rows = patch // pieces

    def hand_out_probe(s, carry):
        piece = piece_of(s, device)
        psum_ref[s] = pacc[:, pl.ds(pl.multiple_of(piece * rows, rows), rows), :].astype(BF16)
        return carry

    lax.fori_loop(0, pieces, hand_out_probe, 0)

def place_kernel(tile_rows, pos_ref, where_ref, grad_ref, *rest):
    *out_refs, sums, grad = rest
    slots = len(out_refs)
    per_holder, _, patch, _ = grad_ref.shape
    width = sums.shape[2]
    block_tiles = (patch + tile_rows - 1) // tile_rows + 1
    first_row = where_ref[slots]
    tall = patch // SUBLANES
    sublane = lax.broadcasted_iota(jnp.int32, (tall + 1, SUBLANES, LANES), 1)
    lanes = lax.broadcasted_iota(jnp.int32, (patch, LANES), 1)
    cols = patch // LANES
    edge = jnp.zeros((1, SUBLANES, LANES), F32)
    for t in range(slots):
        sums[t] = jnp.zeros(sums.shape[1:], BF16)

    def visit(p, carry):
        tile, off, block, lane = place(
            pos_ref[0, p], pos_ref[1, p], first_row, tile_rows, slots, patch, width
        )
        sub = lax.rem(off, SUBLANES)
        base = pl.multiple_of(off - sub, SUBLANES)
        for c in range(2):
            turned = [
                pltpu.roll(grad_ref[p, c, :, q * LANES : (q + 1) * LANES], lax.rem(lane, LANES), 1) for q in range(cols)
            ]
            for q in range(cols + 1):
                here = turned[q] if q < cols else jnp.zeros((patch, LANES), F32)
                before = turned[q - 1] if q > 0 else jnp.zeros((patch, LANES), F32)
                wide = jnp.where(lanes >= lane, here, before).reshape(tall, SUBLANES, LANES)
                wide = pltpu.roll(wide, sub, 1)
                wide = jnp.where(
                    sublane >= sub, jnp.concatenate([wide, edge], axis=0), jnp.concatenate([edge, wide], axis=0)
                )
                grad[c, q] = jnp.zeros(grad.shape[2:], F32)
                grad[c, q, pl.ds(base, patch + SUBLANES), :] = wide.reshape(patch + SUBLANES, LANES)
        for j in range(block_tiles):
            slot = where_ref[tile + j]
            rows = slice(j * tile_rows, (j + 1) * tile_rows)
            for q in range(cols + 1):
                at = pl.ds(pl.multiple_of((block + q) * LANES, LANES), LANES)
                part = jnp.concatenate([grad[0, q, rows], grad[1, q, rows]], axis=0)
                sums[slot, :, at] = (sums[slot, :, at].astype(F32) + part).astype(BF16)
        return carry

    lax.fori_loop(0, per_holder, visit, 0)

    for t in range(slots):
        out_refs[t][...] = sums[t]


def move(value, steps):
    count = lax.axis_size("tile")
    pairs = []
    for i in range(count):
        kind, step = steps[i % 2]
        if kind == "bit":
            to = i ^ step
        else:
            to = i + (step if (i // 2) % 2 == 0 else -step)
        if 0 <= to < count:
            pairs.append((i, to))
    return lax.ppermute(value, "tile", pairs)


def swap_bits(value, bit0, bit1):
    return move(value, (("bit", bit0), ("bit", bit1)))


def to_sibling(value):
    return swap_bits(value, 1, 1)


def piece_of(s, device):
    core = device & 1
    other = s >> (BITS - 1)
    mine = core ^ other
    away0 = sum(((s >> (BITS - 2 - j)) & 1) * bit for j, bit in enumerate(PROBE_BITS[0]))
    away1 = sum(((s >> (BITS - 2 - j)) & 1) * bit for j, bit in enumerate(PROBE_BITS[1]))
    return ((device & (2**BITS - 1)) ^ other) ^ jnp.where(mine == 0, away0, away1)


def place(row, col, first_row, tile_rows, window_tiles, patch, width):
    block_tiles = (patch + tile_rows - 1) // tile_rows + 1
    local_row = row - first_row
    tile = jnp.clip(local_row // tile_rows, 0, window_tiles - block_tiles)
    block = jnp.minimum(col // LANES, (width - patch - LANES) // LANES)
    return tile, local_row - tile * tile_rows, block, col - block * LANES


def pack_kernel(pos_ref, obj_ref, out_ref):
    tile_rows, width = obj_ref.shape[1:]
    both = 2 * tile_rows
    for q in range(width // LANES):
        part = obj_ref[:, :, q * LANES : (q + 1) * LANES].reshape(both, LANES)
        out_ref[q * both : (q + 1) * both] = part.astype(BF16)
    lane = lax.broadcasted_iota(jnp.int32, (HEAD_ROWS, LANES), 1)
    head = jnp.zeros((HEAD_ROWS, LANES), jnp.int32)
    for k in range(2 * pos_ref.shape[1]):
        value = pos_ref[k % 2, k // 2]
        head = jnp.where(lane == 2 * k, value // BASE, head)
        head = jnp.where(lane == 2 * k + 1, lax.rem(value, BASE), head)
    out_ref[width // LANES * both :] = head.astype(F32).astype(BF16)


def coverage_kernel(tile_rows, per_holder, index_ref, heads_ref, probe_ref, out_ref, padded, digits, pos_ref):
    modes, patch = probe_ref.shape[1], probe_ref.shape[2]
    width = out_ref.shape[1]
    slots = heads_ref.shape[0]
    me, count = index_ref[slots], index_ref[slots + 1]
    for s in range(slots):
        digits[s : s + 1] = heads_ref[s].astype(F32)[:1].astype(jnp.int32)
    pltpu.sync_copy(digits, pos_ref)
    total = jnp.zeros((patch, patch), F32)
    for m in range(modes):
        total = total + (probe_ref[0, m] * probe_ref[0, m] + probe_ref[1, m] * probe_ref[1, m])
    padded[...] = jnp.zeros(padded.shape, F32)
    for q in range(patch // LANES):
        padded[q, tile_rows : tile_rows + patch] = total[:, q * LANES : (q + 1) * LANES]
    sublane = lax.broadcasted_iota(jnp.int32, (tile_rows // SUBLANES, SUBLANES, LANES), 1)
    lanes = lax.broadcasted_iota(jnp.int32, (tile_rows, LANES), 1)
    out_ref[...] = jnp.ones(out_ref.shape, F32)

    def shifted(s, p):
        row = pos_ref[s, 4 * p] * BASE + pos_ref[s, 4 * p + 1]
        col = pos_ref[s, 4 * p + 2] * BASE + pos_ref[s, 4 * p + 3]
        holder = index_ref[s]
        there = jnp.logical_and(holder >= 0, holder < count)
        at = jnp.where(there, jnp.clip(me * tile_rows - row + tile_rows, 0, tile_rows + patch), 0)
        block = jnp.minimum(col // LANES, (width - patch - LANES) // LANES)
        lane = col - block * LANES
        sub = lax.rem(at, SUBLANES)
        turned = []
        for q in range(patch // LANES):
            rows = padded[q, pl.ds(pl.multiple_of(at - sub, SUBLANES), tile_rows + SUBLANES), :]
            rows = pltpu.roll(rows.reshape(-1, SUBLANES, LANES), lax.rem(SUBLANES - sub, SUBLANES), 1)
            rows = jnp.where(sublane < SUBLANES - sub, rows[:-1], rows[1:]).reshape(tile_rows, LANES)
            turned.append(pltpu.roll(rows, lax.rem(lane, LANES), 1))
        zero = jnp.zeros((tile_rows, LANES), F32)
        parts = [jnp.where(lanes >= lane, u, v) for u, v in zip(turned + [zero], [zero] + turned)]
        return block, parts

    def visit(s, carry):
        for block, parts in [shifted(s, p) for p in range(per_holder)]:
            for q, part in enumerate(parts):
                cols = pl.ds(pl.multiple_of((block + q) * LANES, LANES), LANES)
                out_ref[:, cols] = out_ref[:, cols] + part
        return carry

    lax.fori_loop(0, slots, visit, 0)


def order_kernel(order_ref, meas_ref, out_ref):
    turn = order_ref[...]
    for p in range(meas_ref.shape[0]):
        rows = jnp.dot(turn, meas_ref[p], preferred_element_type=F32, precision=lax.Precision.HIGHEST)
        turned = lax.dot_general(
            rows, turn, (((1,), (1,)), ((), ())), preferred_element_type=F32, precision=lax.Precision.HIGHEST
        )
        out_ref[p] = jnp.sqrt(turned)


def finish_kernel(index_ref, own_ref, sibling_ref, came_ref, coverage_ref, pieces_ref, object_ref, probe_ref):
    rows = coverage_ref.shape[0]
    inverse = 1.0 / coverage_ref[...]
    for c in range(2):
        at = slice(c * rows, (c + 1) * rows)
        total = own_ref[...].astype(F32)[at] + sibling_ref[...].astype(F32)[at] + came_ref[at]
        object_ref[c] = total * inverse
    piece_rows = pieces_ref.shape[2]
    modes = probe_ref.shape[1]
    for s in range(pieces_ref.shape[0]):
        piece = piece_of(s, index_ref[0])
        at = pl.ds(pl.multiple_of(piece * piece_rows, piece_rows), piece_rows)
        value = pieces_ref[s].astype(F32)
        for c in range(2):
            probe_ref[c, :, at, :] = value[c * modes : (c + 1) * modes]


VMEM = pl.BlockSpec(memory_space=pltpu.VMEM)
SMEM = pl.BlockSpec(memory_space=pltpu.SMEM)


def call(kernel, name, out_shape, in_specs, limit, flops, bytes_accessed, scratch=()):
    return pl.pallas_call(
        kernel,
        out_shape=out_shape,
        in_specs=in_specs,
        out_specs=jax.tree.map(lambda _: VMEM, out_shape),
        scratch_shapes=list(scratch),
        compiler_params=pltpu.CompilerParams(vmem_limit_bytes=limit * MIB),
        cost_estimate=pl.CostEstimate(flops=flops, bytes_accessed=bytes_accessed, transcendentals=0),
        name=name,
    )


def add(a, b):
    return (a.astype(F32) + b.astype(F32)).astype(BF16)


def local(object_field, probe_modes, positions, intensity):
    tile_rows, width = object_field.shape[1:]
    modes, patch = probe_modes.shape[1:3]
    per_holder = positions.shape[0]
    count = lax.axis_size("tile")
    me = lax.axis_index("tile")
    core, chip = me % 2, me // 2
    block_rows = ((patch + tile_rows - 1) // tile_rows + 1) * tile_rows
    both = 2 * tile_rows
    tiles = 2 + 4 * REACH_CHIPS
    first_core = core == 0
    mine_first = positions.T

    own = call(
        pack_kernel, "pack", jax.ShapeDtypeStruct((width // LANES * both + HEAD_ROWS, LANES), BF16), [SMEM, VMEM],
        8, 1_000_000, 1_000_000,
    )(mine_first, object_field)
    pair = list(lax.optimization_barrier((own, to_sibling(own))))
    first = [move(v, (("shift", -4), ("bit", 2))) for v in pair]
    second = [move(jnp.where(first_core, u, v), (("bit", 2), ("shift", 4))) for u, v in zip(first, pair)]
    third = [move(jnp.where(first_core, u, v), (("shift", 4), ("shift", -4))) for u, v in zip(second, first)]
    brought = first + second + third
    window = pair + brought + [to_sibling(v) for v in brought]

    cases = []
    for c in range(2):
        slots = [(0, c), (0, 1 - c)]
        slots += [(away, t) for away in BROUGHT[c] for t in (c, 1 - c)]
        slots += [(away, t) for away in BROUGHT[1 - c] for t in (1 - c, c)]
        order = [(w // 2 - REACH_CHIPS, w % 2) for w in range(tiles)]
        cases.append(
            [
                np.array([away for away, _ in slots]),
                np.array([t for _, t in slots]),
                np.array([slots.index((away, t)) for away, t in order]),
                np.array([slots.index((-away, t)) for away, t in order]),
            ]
        )
    aways, cores, even_where, odd_where = [jnp.where(first_core, u, v) for u, v in zip(*cases, strict=True)]
    even = chip % 2 == 0
    holders = 2 * (chip + jnp.where(even, aways, -aways)) + cores
    index = jnp.concatenate([holders, me[None], jnp.full((1,), count)]).astype(jnp.int32)
    first_row = (2 * (chip - REACH_CHIPS)) * tile_rows
    where = jnp.concatenate([jnp.where(even, even_where, odd_where), first_row[None], me[None]]).astype(jnp.int32)

    right, left = real_tables(patch)
    ordered = call(
        order_kernel, "order", jax.ShapeDtypeStruct(intensity.shape, F32), [VMEM, VMEM], 8, 2_000_000_000, 2_000_000
    )(jnp.asarray(frequency_order(patch)), lax.optimization_barrier((intensity, first[0]))[0])

    pieces = 2**BITS
    rows = patch // pieces
    planes = 2 * modes + 1
    cols = patch // LANES
    grads, psum = call(
        lambda *refs: positions_kernel(tile_rows, *refs), "positions",
        (
            jax.ShapeDtypeStruct((per_holder, 2, patch, patch), F32),
            jax.ShapeDtypeStruct((pieces, planes, rows, patch), BF16),
        ),
        [SMEM, SMEM, VMEM, VMEM, VMEM, VMEM, VMEM],
        16, 10_000_000_000, 12_000_000,
        [
            pltpu.VMEM((2, cols + 1, block_rows + 16, LANES), F32),
            pltpu.VMEM((2, patch, patch), F32),
            pltpu.VMEM((2, modes, patch, patch), F32),
            pltpu.VMEM((modes, patch, 2 * patch), BF16),
            pltpu.VMEM((planes, patch, patch), F32),
        ],
    )(mine_first, where, jnp.stack(window), probe_modes, ordered, right, left)
    (a0, b0, c0), (a1, b1, c1) = PROBE_BITS
    psum = psum.reshape((2,) * BITS + (planes, rows, patch))
    psum = add(psum[0], to_sibling(psum[1]))
    psum_came = swap_bits(psum[1], a0, a1)
    grads = lax.optimization_barrier((grads, psum))[0]
    sums = call(
        lambda *refs: place_kernel(tile_rows, *refs), "place",
        (jax.ShapeDtypeStruct((both, width), BF16),) * tiles,
        [SMEM, SMEM, VMEM],
        16, 1_000_000_000, 12_000_000,
        [
            pltpu.VMEM((tiles, both, width), BF16),
            pltpu.VMEM((2, cols + 1, block_rows + 16, LANES), F32),
        ],
    )(mine_first, where, grads)

    own_sum, sibling_sum, *sums = sums
    kept, given = sums[: 2 * REACH_CHIPS], list(sums[2 * REACH_CHIPS :])
    sums = [None] * 2 * REACH_CHIPS
    for j in (5, 4, 3, 2, 1, 0):
        if j < 4:
            given[j] = lax.optimization_barrier((given[j], sums[j + 2]))[0]
        sums[j] = add(kept[j], to_sibling(given[j]))
    psum = add(psum[0], psum_came)
    sums[5], sums[4], psum = lax.optimization_barrier((sums[5], sums[4], psum))
    heads, _ = lax.optimization_barrier((jnp.stack([v[-HEAD_ROWS:] for v in window]), sums[5]))
    coverage = call(
        lambda *refs: coverage_kernel(tile_rows, per_holder, *refs), "coverage",
        jax.ShapeDtypeStruct((tile_rows, width), F32), [SMEM, VMEM, VMEM],
        8, 10_000_000, 3_000_000,
        [
            pltpu.VMEM((patch // LANES, patch + 2 * tile_rows + 16, LANES), F32),
            pltpu.VMEM((16, LANES), jnp.int32),
            pltpu.SMEM((16, LANES), jnp.int32),
        ],
    )(index, heads, probe_modes)

    came3 = [move(sums[4 + j], (("shift", -4), ("shift", 4))) for j in (1, 0)]
    sum2 = [add(sums[2 + j], jnp.where(first_core, v, 0)) for j, v in zip((1, 0), came3)]
    came2 = [move(v, (("bit", 2), ("shift", -4))) for v in sum2]
    sum1 = [add(sums[j], jnp.where(first_core, u, v)) for j, u, v in zip((1, 0), came2, came3)]
    came1 = [move(v, (("shift", 4), ("bit", 2))) for v in sum1]
    came = [u.astype(F32) + jnp.where(first_core, 0, v).astype(F32) for u, v in zip(came1, came2)]
    from_sibling = to_sibling((sibling_sum.astype(F32) + came[0]).astype(BF16))
    def after(value, *others):
        return lax.optimization_barrier((value, *others))[0]

    psum = add(psum, swap_bits(psum, b0, b1)[::-1])
    psum = after(psum, came3[0], coverage)
    psum = add(psum, swap_bits(psum, c0, c1)[:, ::-1])
    bit = 1 << BITS
    while bit < count:
        psum = add(psum, swap_bits(psum, bit, bit))
        bit *= 2
    psum = psum.astype(F32)
    pstep = (psum[:, :, : 2 * modes] / jnp.sqrt(1.0 + psum[:, :, 2 * modes :])).astype(BF16)
    pstep = after(pstep, came2[0])
    pstep = jnp.stack([pstep, swap_bits(pstep, a0, a1)])
    pstep = jnp.stack([pstep, to_sibling(pstep)])
    return call(
        finish_kernel, "finish",
        (jax.ShapeDtypeStruct(object_field.shape, F32), jax.ShapeDtypeStruct(probe_modes.shape, F32)),
        [SMEM] + [VMEM] * 5, 16, 2_000_000, 6_000_000,
    )(
        me[None].astype(jnp.int32), own_sum, from_sibling, came[1], coverage,
        pstep.reshape(pieces, 2 * modes, rows, patch),
    )


def solution(mesh):
    in_specs = (
        P(None, ("grp", "tile"), None),
        P(None, "grp", None, None),
        P(("grp", "tile"), None),
        P(("grp", "tile"), None, None),
    )
    out_specs = (P(None, ("grp", "tile"), None), P(None, "grp", None, None))
    return jax.shard_map(local, mesh=mesh, in_specs=in_specs, out_specs=out_specs, check_vma=False)
```

```python
import math

import jax
import jax.numpy as jnp
import numpy as np
from jax import lax
from jax.experimental import pallas as pl
from jax.experimental.pallas import tpu as pltpu
from jax.sharding import PartitionSpec as P

F32 = jnp.float32
BF16 = jnp.bfloat16
LANES = 128
SUBLANES = 8
MIB = 1024 * 1024
BROUGHT = ((2, -1, -3), (1, -2, 3))
REACH_CHIPS = 3
PROBE_BITS = ((2, 4, 8), (4, 8, 2))
BITS = 4
HEAD_ROWS = 16
BASE = 128
CHUNK = 32


def real_tables(size):
    steps = np.arange(size)
    phase = (steps[:, None] * steps[None, :] % size) * (2.0 * math.pi / size)
    factor = 1.0 / math.sqrt(size)
    cos_table, sine_table = np.cos(phase) * factor, np.sin(phase) * factor
    mid = size // 2
    table = np.concatenate([cos_table[:, :mid], cos_table[:, mid : mid + 1], sine_table[:, 1:mid]], axis=1)
    return jnp.asarray(table, BF16), jnp.asarray(table.T.copy(), BF16)


def frequency_order(size):
    mid = size // 2
    order = np.concatenate([np.arange(mid), [mid], np.arange(size - 1, mid, -1)])
    return np.eye(size, dtype=np.float32)[order]


def dot(a, b):
    return jnp.dot(a, b, preferred_element_type=F32)


def with_first_row(first, rest):
    row = lax.broadcasted_iota(jnp.int32, (SUBLANES, rest.shape[1]), 0)
    top = jnp.where(row == 0, first[:SUBLANES], rest[:SUBLANES])
    return jnp.concatenate([top, rest[SUBLANES:]], axis=0)


def with_first_lane(first, rest):
    lane = lax.broadcasted_iota(jnp.int32, rest.shape, 1)
    return jnp.where(lane == 0, first, rest)


def unfold(pick, axis, u, v):
    mid = u.shape[axis] // 2
    part = (lambda x, i: x[i * mid : (i + 1) * mid]) if axis == 0 else (lambda x, i: x[:, i * mid : (i + 1) * mid])
    u1, u2, v1, v2 = part(u, 0), part(u, 1), part(v, 0), part(v, 1)
    real = jnp.concatenate([pick(u1, u1 + v2), pick(u2, u1 - v2)], axis=axis)
    imag = jnp.concatenate([pick(v1, v1 - u2), pick(v2, v1 + u2)], axis=axis)
    return real, imag


def fold(pick, axis, real, imag):
    mid = real.shape[axis] // 2
    part = (lambda x, i: x[i * mid : (i + 1) * mid]) if axis == 0 else (lambda x, i: x[:, i * mid : (i + 1) * mid])
    r1, r2, i1, i2 = part(real, 0), part(real, 1), part(imag, 0), part(imag, 1)
    a = jnp.concatenate([pick(r1, r1 + r2), pick(r2, i2 - i1)], axis=axis)
    b = jnp.concatenate([pick(i1, i1 + i2), pick(i2, r1 - r2)], axis=axis)
    return a.astype(BF16), b.astype(BF16)


def positions_kernel(
    tile_rows, pos_ref, where_ref, win_ref, probe_ref, meas_ref, right_ref, left_ref,
    grad_ref, psum_ref, raw, obj, far, half, pacc,
):
    slots = win_ref.shape[0]
    per_holder = meas_ref.shape[0]
    modes = probe_ref.shape[1]
    patch = probe_ref.shape[2]
    both = 2 * tile_rows
    width = win_ref.shape[1] // both * LANES
    block_tiles = (patch + tile_rows - 1) // tile_rows + 1
    first_row = where_ref[slots]
    device = where_ref[slots + 1]
    tall = patch // SUBLANES
    sublane = lax.broadcasted_iota(jnp.int32, (tall, SUBLANES, LANES), 1)
    lanes = lax.broadcasted_iota(jnp.int32, (patch, LANES), 1)
    cols = patch // LANES
    pacc[...] = jnp.zeros(pacc.shape, F32)

    def visit(p, carry):
        tile, off, block, lane = place(
            pos_ref[0, p], pos_ref[1, p], first_row, tile_rows, slots, patch, width
        )
        sub = lax.rem(off, SUBLANES)
        base = pl.multiple_of(off - sub, SUBLANES)
        for j in range(block_tiles):
            for q in range(cols + 1):
                at = pl.ds(pl.multiple_of((block + q) * both, 16), both)
                part = win_ref[where_ref[tile + j], at, :].astype(F32)
                raw[0, q, j * tile_rows : (j + 1) * tile_rows] = part[:tile_rows]
                raw[1, q, j * tile_rows : (j + 1) * tile_rows] = part[tile_rows:]
        for c in range(2):
            turned = []
            for q in range(cols + 1):
                rows = raw[c, q, pl.ds(base, patch + SUBLANES), :].reshape(tall + 1, SUBLANES, LANES)
                rows = pltpu.roll(rows, lax.rem(SUBLANES - sub, SUBLANES), 1)
                rows = jnp.where(sublane < SUBLANES - sub, rows[:tall], rows[1:])
                turned.append(pltpu.roll(rows.reshape(patch, LANES), lax.rem(LANES - lane, LANES), 1))
            for q in range(cols):
                obj[c, :, q * LANES : (q + 1) * LANES] = jnp.where(lanes < LANES - lane, turned[q], turned[q + 1])
        pacc[2 * modes] = pacc[2 * modes] + (obj[0] * obj[0] + obj[1] * obj[1])
        for i in range(patch // CHUNK):
            at = slice(i * CHUNK, (i + 1) * CHUNK)
            obj_real, obj_imag = obj[0, at, :], obj[1, at, :]
            exits = []
            for m in range(modes):
                probe_real, probe_imag = probe_ref[0, m, at, :], probe_ref[1, m, at, :]
                exits.append((probe_real * obj_real - probe_imag * obj_imag).astype(BF16))
                exits.append((probe_real * obj_imag + probe_imag * obj_real).astype(BF16))
            out = dot(jnp.concatenate(exits, axis=0), right_ref[...])
            for m in range(modes):
                u, v = [out[(2 * m + j) * CHUNK : (2 * m + j + 1) * CHUNK] for j in range(2)]
                real, imag = unfold(with_first_lane, 1, u, v)
                half[m, at, :patch] = real.astype(BF16)
                half[m, at, patch:] = imag.astype(BF16)
        for m in range(modes):
            out = dot(left_ref[...], half[m])
            far[0, m], far[1, m] = unfold(with_first_row, 0, out[:, :patch], out[:, patch:])
        mid = patch // 2

        def both_halves(ref, lead, start, cols=slice(None)):
            low, high = [ref[(*lead, slice(at, at + CHUNK // 2), cols)] for at in (start, start + mid)]
            return jnp.concatenate([low, high], axis=0)

        for start in range(0, mid, CHUNK // 2):
            fars = [(both_halves(far, (0, m), start), both_halves(far, (1, m), start)) for m in range(modes)]
            model = 1.0 + sum(r * r + i * i for r, i in fars)
            factor = both_halves(meas_ref, (p,), start) * lax.rsqrt(model) - 1.0
            folded = []
            for r, i in fars:
                folded += fold(with_first_lane, 1, r * factor, i * factor)
            out = dot(jnp.concatenate(folded, axis=0), left_ref[...])

            pick = with_first_row if start == 0 else lambda top, rest: rest
            low, high = slice(start, start + CHUNK // 2), slice(start + mid, start + mid + CHUNK // 2)
            for m in range(modes):
                u, v = [out[(2 * m + j) * CHUNK : (2 * m + j + 1) * CHUNK] for j in range(2)]
                for part, side in zip(fold(pick, 0, u, v), (slice(0, patch), slice(patch, None)), strict=True):
                    half[m, low, side], half[m, high, side] = part[: CHUNK // 2], part[CHUNK // 2 :]
        for m in range(modes):
            out = dot(right_ref[...], half[m])
            far[0, m] = out[:, :patch]
            far[1, m] = out[:, patch:]

        for i in range(patch // CHUNK):
            at = slice(i * CHUNK, (i + 1) * CHUNK)
            obj_real, obj_imag = obj[0, at, :], obj[1, at, :]
            grad_real = jnp.zeros((CHUNK, patch), F32)
            grad_imag = jnp.zeros((CHUNK, patch), F32)
            for m in range(modes):
                change_real, change_imag = far[0, m, at, :], far[1, m, at, :]
                probe_real, probe_imag = probe_ref[0, m, at, :], probe_ref[1, m, at, :]
                grad_real = grad_real + (probe_real * change_real + probe_imag * change_imag)
                grad_imag = grad_imag + (probe_real * change_imag - probe_imag * change_real)
                pacc[m, at, :] = pacc[m, at, :] + (obj_real * change_real + obj_imag * change_imag)
                pacc[modes + m, at, :] = pacc[modes + m, at, :] + (obj_real * change_imag - obj_imag * change_real)
            grad_ref[p, 0, at, :] = grad_real
            grad_ref[p, 1, at, :] = grad_imag
        return carry

    lax.fori_loop(0, per_holder, visit, 0)

    pieces = psum_ref.shape[0]
    rows = patch // pieces

    def hand_out_probe(s, carry):
        piece = piece_of(s, device)
        psum_ref[s] = pacc[:, pl.ds(pl.multiple_of(piece * rows, rows), rows), :].astype(BF16)
        return carry

    lax.fori_loop(0, pieces, hand_out_probe, 0)

def place_kernel(tile_rows, pos_ref, where_ref, grad_ref, *rest):
    *out_refs, sums, grad = rest
    slots = len(out_refs)
    per_holder, _, patch, _ = grad_ref.shape
    width = sums.shape[2]
    block_tiles = (patch + tile_rows - 1) // tile_rows + 1
    first_row = where_ref[slots]
    tall = patch // SUBLANES
    sublane = lax.broadcasted_iota(jnp.int32, (tall + 1, SUBLANES, LANES), 1)
    lanes = lax.broadcasted_iota(jnp.int32, (patch, LANES), 1)
    cols = patch // LANES
    edge = jnp.zeros((1, SUBLANES, LANES), F32)
    for t in range(slots):
        sums[t] = jnp.zeros(sums.shape[1:], BF16)

    def visit(p, carry):
        tile, off, block, lane = place(
            pos_ref[0, p], pos_ref[1, p], first_row, tile_rows, slots, patch, width
        )
        sub = lax.rem(off, SUBLANES)
        base = pl.multiple_of(off - sub, SUBLANES)
        for c in range(2):
            turned = [
                pltpu.roll(grad_ref[p, c, :, q * LANES : (q + 1) * LANES], lax.rem(lane, LANES), 1) for q in range(cols)
            ]
            for q in range(cols + 1):
                here = turned[q] if q < cols else jnp.zeros((patch, LANES), F32)
                before = turned[q - 1] if q > 0 else jnp.zeros((patch, LANES), F32)
                wide = jnp.where(lanes >= lane, here, before).reshape(tall, SUBLANES, LANES)
                wide = pltpu.roll(wide, sub, 1)
                wide = jnp.where(
                    sublane >= sub, jnp.concatenate([wide, edge], axis=0), jnp.concatenate([edge, wide], axis=0)
                )
                grad[c, q] = jnp.zeros(grad.shape[2:], F32)
                grad[c, q, pl.ds(base, patch + SUBLANES), :] = wide.reshape(patch + SUBLANES, LANES)
        for j in range(block_tiles):
            slot = where_ref[tile + j]
            rows = slice(j * tile_rows, (j + 1) * tile_rows)
            for q in range(cols + 1):
                at = pl.ds(pl.multiple_of((block + q) * LANES, LANES), LANES)
                part = jnp.concatenate([grad[0, q, rows], grad[1, q, rows]], axis=0)
                sums[slot, :, at] = (sums[slot, :, at].astype(F32) + part).astype(BF16)
        return carry

    lax.fori_loop(0, per_holder, visit, 0)

    for t in range(slots):
        out_refs[t][...] = sums[t]


def move(value, steps):
    count = lax.axis_size("tile")
    pairs = []
    for i in range(count):
        kind, step = steps[i % 2]
        if kind == "bit":
            to = i ^ step
        else:
            to = i + (step if (i // 2) % 2 == 0 else -step)
        if 0 <= to < count:
            pairs.append((i, to))
    return lax.ppermute(value, "tile", pairs)


def swap_bits(value, bit0, bit1):
    return move(value, (("bit", bit0), ("bit", bit1)))


def to_sibling(value):
    return swap_bits(value, 1, 1)


def piece_of(s, device):
    core = device & 1
    other = s >> (BITS - 1)
    mine = core ^ other
    away0 = sum(((s >> (BITS - 2 - j)) & 1) * bit for j, bit in enumerate(PROBE_BITS[0]))
    away1 = sum(((s >> (BITS - 2 - j)) & 1) * bit for j, bit in enumerate(PROBE_BITS[1]))
    return ((device & (2**BITS - 1)) ^ other) ^ jnp.where(mine == 0, away0, away1)


def place(row, col, first_row, tile_rows, window_tiles, patch, width):
    block_tiles = (patch + tile_rows - 1) // tile_rows + 1
    local_row = row - first_row
    tile = jnp.clip(local_row // tile_rows, 0, window_tiles - block_tiles)
    block = jnp.minimum(col // LANES, (width - patch - LANES) // LANES)
    return tile, local_row - tile * tile_rows, block, col - block * LANES


def pack_kernel(pos_ref, obj_ref, out_ref):
    tile_rows, width = obj_ref.shape[1:]
    both = 2 * tile_rows
    for q in range(width // LANES):
        part = obj_ref[:, :, q * LANES : (q + 1) * LANES].reshape(both, LANES)
        out_ref[q * both : (q + 1) * both] = part.astype(BF16)
    lane = lax.broadcasted_iota(jnp.int32, (HEAD_ROWS, LANES), 1)
    head = jnp.zeros((HEAD_ROWS, LANES), jnp.int32)
    for k in range(2 * pos_ref.shape[1]):
        value = pos_ref[k % 2, k // 2]
        head = jnp.where(lane == 2 * k, value // BASE, head)
        head = jnp.where(lane == 2 * k + 1, lax.rem(value, BASE), head)
    out_ref[width // LANES * both :] = head.astype(F32).astype(BF16)


def coverage_kernel(tile_rows, per_holder, index_ref, heads_ref, probe_ref, out_ref, padded, digits, pos_ref):
    modes, patch = probe_ref.shape[1], probe_ref.shape[2]
    width = out_ref.shape[1]
    slots = heads_ref.shape[0]
    me, count = index_ref[slots], index_ref[slots + 1]
    for s in range(slots):
        digits[s : s + 1] = heads_ref[s].astype(F32)[:1].astype(jnp.int32)
    pltpu.sync_copy(digits, pos_ref)
    total = jnp.zeros((patch, patch), F32)
    for m in range(modes):
        total = total + (probe_ref[0, m] * probe_ref[0, m] + probe_ref[1, m] * probe_ref[1, m])
    padded[...] = jnp.zeros(padded.shape, F32)
    for q in range(patch // LANES):
        padded[q, tile_rows : tile_rows + patch] = total[:, q * LANES : (q + 1) * LANES]
    sublane = lax.broadcasted_iota(jnp.int32, (tile_rows // SUBLANES, SUBLANES, LANES), 1)
    lanes = lax.broadcasted_iota(jnp.int32, (tile_rows, LANES), 1)
    out_ref[...] = jnp.ones(out_ref.shape, F32)

    def shifted(s, p):
        row = pos_ref[s, 4 * p] * BASE + pos_ref[s, 4 * p + 1]
        col = pos_ref[s, 4 * p + 2] * BASE + pos_ref[s, 4 * p + 3]
        holder = index_ref[s]
        there = jnp.logical_and(holder >= 0, holder < count)
        at = jnp.where(there, jnp.clip(me * tile_rows - row + tile_rows, 0, tile_rows + patch), 0)
        block = jnp.minimum(col // LANES, (width - patch - LANES) // LANES)
        lane = col - block * LANES
        sub = lax.rem(at, SUBLANES)
        turned = []
        for q in range(patch // LANES):
            rows = padded[q, pl.ds(pl.multiple_of(at - sub, SUBLANES), tile_rows + SUBLANES), :]
            rows = pltpu.roll(rows.reshape(-1, SUBLANES, LANES), lax.rem(SUBLANES - sub, SUBLANES), 1)
            rows = jnp.where(sublane < SUBLANES - sub, rows[:-1], rows[1:]).reshape(tile_rows, LANES)
            turned.append(pltpu.roll(rows, lax.rem(lane, LANES), 1))
        zero = jnp.zeros((tile_rows, LANES), F32)
        parts = [jnp.where(lanes >= lane, u, v) for u, v in zip(turned + [zero], [zero] + turned)]
        return block, parts

    def visit(s, carry):
        for block, parts in [shifted(s, p) for p in range(per_holder)]:
            for q, part in enumerate(parts):
                cols = pl.ds(pl.multiple_of((block + q) * LANES, LANES), LANES)
                out_ref[:, cols] = out_ref[:, cols] + part
        return carry

    lax.fori_loop(0, slots, visit, 0)


def order_kernel(order_ref, meas_ref, out_ref):
    turn = order_ref[...]
    for p in range(meas_ref.shape[0]):
        rows = jnp.dot(turn, meas_ref[p], preferred_element_type=F32, precision=lax.Precision.HIGHEST)
        turned = lax.dot_general(
            rows, turn, (((1,), (1,)), ((), ())), preferred_element_type=F32, precision=lax.Precision.HIGHEST
        )
        out_ref[p] = jnp.sqrt(turned)


def finish_kernel(index_ref, own_ref, sibling_ref, came_ref, coverage_ref, pieces_ref, object_ref, probe_ref):
    rows = coverage_ref.shape[0]
    inverse = 1.0 / coverage_ref[...]
    for c in range(2):
        at = slice(c * rows, (c + 1) * rows)
        total = own_ref[...].astype(F32)[at] + sibling_ref[...].astype(F32)[at] + came_ref[at]
        object_ref[c] = total * inverse
    piece_rows = pieces_ref.shape[2]
    modes = probe_ref.shape[1]
    for s in range(pieces_ref.shape[0]):
        piece = piece_of(s, index_ref[0])
        at = pl.ds(pl.multiple_of(piece * piece_rows, piece_rows), piece_rows)
        value = pieces_ref[s].astype(F32)
        for c in range(2):
            probe_ref[c, :, at, :] = value[c * modes : (c + 1) * modes]


VMEM = pl.BlockSpec(memory_space=pltpu.VMEM)
SMEM = pl.BlockSpec(memory_space=pltpu.SMEM)


def call(kernel, name, out_shape, in_specs, limit, flops, bytes_accessed, scratch=()):
    return pl.pallas_call(
        kernel,
        out_shape=out_shape,
        in_specs=in_specs,
        out_specs=jax.tree.map(lambda _: VMEM, out_shape),
        scratch_shapes=list(scratch),
        compiler_params=pltpu.CompilerParams(vmem_limit_bytes=limit * MIB),
        cost_estimate=pl.CostEstimate(flops=flops, bytes_accessed=bytes_accessed, transcendentals=0),
        name=name,
    )


def add(a, b):
    return (a.astype(F32) + b.astype(F32)).astype(BF16)


def local(object_field, probe_modes, positions, intensity):
    tile_rows, width = object_field.shape[1:]
    modes, patch = probe_modes.shape[1:3]
    per_holder = positions.shape[0]
    count = lax.axis_size("tile")
    me = lax.axis_index("tile")
    core, chip = me % 2, me // 2
    block_rows = ((patch + tile_rows - 1) // tile_rows + 1) * tile_rows
    both = 2 * tile_rows
    tiles = 2 + 4 * REACH_CHIPS
    first_core = core == 0
    mine_first = positions.T

    own = call(
        pack_kernel, "pack", jax.ShapeDtypeStruct((width // LANES * both + HEAD_ROWS, LANES), BF16), [SMEM, VMEM],
        8, 1_000_000, 1_000_000,
    )(mine_first, object_field)
    pair = list(lax.optimization_barrier((own, to_sibling(own))))
    first = [move(v, (("shift", -4), ("bit", 2))) for v in pair]
    second = [move(jnp.where(first_core, u, v), (("bit", 2), ("shift", 4))) for u, v in zip(first, pair)]
    third = [move(jnp.where(first_core, u, v), (("shift", 4), ("shift", -4))) for u, v in zip(second, first)]
    brought = first + second + third
    window = pair + brought + [to_sibling(v) for v in brought]

    cases = []
    for c in range(2):
        slots = [(0, c), (0, 1 - c)]
        slots += [(away, t) for away in BROUGHT[c] for t in (c, 1 - c)]
        slots += [(away, t) for away in BROUGHT[1 - c] for t in (1 - c, c)]
        order = [(w // 2 - REACH_CHIPS, w % 2) for w in range(tiles)]
        cases.append(
            [
                np.array([away for away, _ in slots]),
                np.array([t for _, t in slots]),
                np.array([slots.index((away, t)) for away, t in order]),
                np.array([slots.index((-away, t)) for away, t in order]),
            ]
        )
    aways, cores, even_where, odd_where = [jnp.where(first_core, u, v) for u, v in zip(*cases, strict=True)]
    even = chip % 2 == 0
    holders = 2 * (chip + jnp.where(even, aways, -aways)) + cores
    index = jnp.concatenate([holders, me[None], jnp.full((1,), count)]).astype(jnp.int32)
    first_row = (2 * (chip - REACH_CHIPS)) * tile_rows
    where = jnp.concatenate([jnp.where(even, even_where, odd_where), first_row[None], me[None]]).astype(jnp.int32)

    right, left = real_tables(patch)
    ordered = call(
        order_kernel, "order", jax.ShapeDtypeStruct(intensity.shape, F32), [VMEM, VMEM], 8, 2_000_000_000, 2_000_000
    )(jnp.asarray(frequency_order(patch)), lax.optimization_barrier((intensity, second[1]))[0])

    pieces = 2**BITS
    rows = patch // pieces
    planes = 2 * modes + 1
    cols = patch // LANES
    grads, psum = call(
        lambda *refs: positions_kernel(tile_rows, *refs), "positions",
        (
            jax.ShapeDtypeStruct((per_holder, 2, patch, patch), F32),
            jax.ShapeDtypeStruct((pieces, planes, rows, patch), BF16),
        ),
        [SMEM, SMEM, VMEM, VMEM, VMEM, VMEM, VMEM],
        16, 10_000_000_000, 12_000_000,
        [
            pltpu.VMEM((2, cols + 1, block_rows + 16, LANES), F32),
            pltpu.VMEM((2, patch, patch), F32),
            pltpu.VMEM((2, modes, patch, patch), F32),
            pltpu.VMEM((modes, patch, 2 * patch), BF16),
            pltpu.VMEM((planes, patch, patch), F32),
        ],
    )(mine_first, where, jnp.stack(window), probe_modes, ordered, right, left)
    (a0, b0, c0), (a1, b1, c1) = PROBE_BITS
    psum = psum.reshape((2,) * BITS + (planes, rows, patch))
    psum = add(psum[0], to_sibling(psum[1]))
    psum_came = swap_bits(psum[1], a0, a1)
    grads = lax.optimization_barrier((grads, psum))[0]
    sums = call(
        lambda *refs: place_kernel(tile_rows, *refs), "place",
        (jax.ShapeDtypeStruct((both, width), BF16),) * tiles,
        [SMEM, SMEM, VMEM],
        16, 1_000_000_000, 12_000_000,
        [
            pltpu.VMEM((tiles, both, width), BF16),
            pltpu.VMEM((2, cols + 1, block_rows + 16, LANES), F32),
        ],
    )(mine_first, where, grads)

    own_sum, sibling_sum, *sums = sums
    kept, given = sums[: 2 * REACH_CHIPS], list(sums[2 * REACH_CHIPS :])
    sums = [None] * 2 * REACH_CHIPS
    for j in (5, 4, 3, 2, 1, 0):
        if j < 4:
            given[j] = lax.optimization_barrier((given[j], sums[j + 2]))[0]
        sums[j] = add(kept[j], to_sibling(given[j]))
    psum = add(psum[0], psum_came)
    sums[5], sums[4], psum = lax.optimization_barrier((sums[5], sums[4], psum))
    heads, _ = lax.optimization_barrier((jnp.stack([v[-HEAD_ROWS:] for v in window]), sums[5]))
    coverage = call(
        lambda *refs: coverage_kernel(tile_rows, per_holder, *refs), "coverage",
        jax.ShapeDtypeStruct((tile_rows, width), F32), [SMEM, VMEM, VMEM],
        8, 10_000_000, 3_000_000,
        [
            pltpu.VMEM((patch // LANES, patch + 2 * tile_rows + 16, LANES), F32),
            pltpu.VMEM((16, LANES), jnp.int32),
            pltpu.SMEM((16, LANES), jnp.int32),
        ],
    )(index, heads, probe_modes)

    came3 = [move(sums[4 + j], (("shift", -4), ("shift", 4))) for j in (1, 0)]
    sum2 = [add(sums[2 + j], jnp.where(first_core, v, 0)) for j, v in zip((1, 0), came3)]
    came2 = [move(v, (("bit", 2), ("shift", -4))) for v in sum2]
    sum1 = [add(sums[j], jnp.where(first_core, u, v)) for j, u, v in zip((1, 0), came2, came3)]
    came1 = [move(v, (("shift", 4), ("bit", 2))) for v in sum1]
    came = [u.astype(F32) + jnp.where(first_core, 0, v).astype(F32) for u, v in zip(came1, came2)]
    from_sibling = to_sibling((sibling_sum.astype(F32) + came[0]).astype(BF16))
    def after(value, *others):
        return lax.optimization_barrier((value, *others))[0]

    psum = add(psum, swap_bits(psum, b0, b1)[::-1])
    psum = after(psum, came3[0], coverage)
    psum = add(psum, swap_bits(psum, c0, c1)[:, ::-1])
    bit = 1 << BITS
    while bit < count:
        psum = add(psum, swap_bits(psum, bit, bit))
        bit *= 2
    psum = psum.astype(F32)
    pstep = (psum[:, :, : 2 * modes] / jnp.sqrt(1.0 + psum[:, :, 2 * modes :])).astype(BF16)
    pstep = after(pstep, came2[0])
    pstep = jnp.stack([pstep, swap_bits(pstep, a0, a1)])
    pstep = jnp.stack([pstep, to_sibling(pstep)])
    return call(
        finish_kernel, "finish",
        (jax.ShapeDtypeStruct(object_field.shape, F32), jax.ShapeDtypeStruct(probe_modes.shape, F32)),
        [SMEM] + [VMEM] * 5, 16, 2_000_000, 6_000_000,
    )(
        me[None].astype(jnp.int32), own_sum, from_sibling, came[1], coverage,
        pstep.reshape(pieces, 2 * modes, rows, patch),
    )


def solution(mesh):
    in_specs = (
        P(None, ("grp", "tile"), None),
        P(None, "grp", None, None),
        P(("grp", "tile"), None),
        P(("grp", "tile"), None, None),
    )
    out_specs = (P(None, ("grp", "tile"), None), P(None, "grp", None, None))
    return jax.shard_map(local, mesh=mesh, in_specs=in_specs, out_specs=out_specs, check_vma=False)
```
